128 devices in a mesh: grid: 16 (over z, x), band: 8 (over y, core).
Axes of the slice: x: 4, y: 4, z: 4, core: 2. Of those that a mesh axis runs over, the one named last changes fastest.
Arguments:
- orbitals: bfloat16 [16384, 12288], P('grid', 'band'), may hold values from -1.1953125 to 1.1953125
- point_owner: int32 [4096, 1], replicated, may hold values from 0 to 15; in each aligned block of 256 rows (0 to 255, 256 to 511, ...) at most 32 rows name the same one
- point_row: int32 [4096], replicated, may hold values from 0 to 1023
- density_tiles: bfloat16 [24, 6, 512, 512], P('band'), as said below
- tile_columns: int32 [24, 6], P('band'), may hold values from 0 to 23, as said below
- tile_counts: int32 [24], P('band'), may hold values from 1 to 6, as said below
Outputs:
- exchange_rows: bfloat16 [4096, 12288], P('grid', 'band')
The draws below stay inside these ranges and needn't reach their ends.
Inputs may be any that keep to these rules, and one draw needn't show every extreme that they name: `point_owner`: among the 256 points of each aligned block, no grid index is named more than 32 times, and some grid index is named exactly 32 times in every block. `tile_columns`: row r lists r first and then distinct tile columns; the first tile_counts[r] entries are the stored nonzero tiles. The pattern is symmetric: column c is in use in row r exactly when r is in use in row c. `tile_counts`: some tile row uses all 6 slots in every draw. `density_tiles`: the density matrix is symmetric: the tile stored in row r for column c is the transpose of the tile stored in row c for column r.
All inputs are finite; a program needn't handle non-finite values.
Results may differ from the reference program's by a relative error of at most 0.0056.
Values may be sent and summed in bfloat16 or wider, within the bound.
A program may use at most 128 MiB of HBM per device.

```python
import math
import jax
import jax.numpy as jnp
import numpy as np
from jax import lax

NORB = 12288
TILE = 512
KT = 6
P_DEV = 256
GRID_DEV = 1024
NPTS = 4096
NGRID = 16384
CAP = 32
NTR = 24
N_GRID = 16


def tile_pattern(key):
    order = jax.random.permutation(jax.random.fold_in(key, 11), NTR).astype(jnp.int32)
    where = jnp.argsort(order).astype(jnp.int32)
    coins = jax.random.randint(jax.random.fold_in(key, 12), (KT - 1, NTR), 0, 2)
    rounds = jnp.arange(1, KT, dtype=jnp.int32)
    position = where[:, None]
    other = jnp.bitwise_xor(position, rounds[None, :])
    lowest = jnp.minimum(position, other)
    kept = (coins[rounds[None, :] - 1, lowest] == 1) | (lowest == 0)
    partner = order[other]
    ranking = jnp.where(kept, rounds[None, :], KT + rounds[None, :])
    slot_order = jnp.argsort(ranking, axis=1, stable=True)
    partner = jnp.take_along_axis(partner, slot_order, axis=1)
    columns = jnp.concatenate([jnp.arange(NTR, dtype=jnp.int32)[:, None], partner], axis=1).astype(jnp.int32)
    counts = (1 + jnp.sum(kept.astype(jnp.int32), axis=1)).astype(jnp.int32)
    return (columns, counts)


def draw_tile_columns(key, part):
    columns, counts = tile_pattern(key)
    return columns


def draw_tile_counts(key, part):
    columns, counts = tile_pattern(key)
    return counts


def draw_density_tiles(key, part):
    columns, counts = tile_pattern(key)
    key = jax.random.fold_in(key, 3)
    row_ids = jnp.broadcast_to(jnp.arange(NTR, dtype=jnp.int32)[:, None], (NTR, KT))
    lowest = jnp.minimum(row_ids, columns).reshape(-1)
    highest = jnp.maximum(row_ids, columns).reshape(-1)
    keys = jax.vmap(jax.random.fold_in, in_axes=(None, 0))(key, lowest * NTR + highest)
    bases = jax.vmap(lambda sub: jax.random.normal(sub, (TILE, TILE), jnp.float32))(keys)
    flipped = jnp.swapaxes(bases, 1, 2)
    mirrored = (bases + flipped) * 0.7071
    row_flat = row_ids.reshape(-1)[:, None, None]
    col_flat = columns.reshape(-1)[:, None, None]
    values = jnp.where(row_flat == col_flat, mirrored, jnp.where(row_flat < col_flat, bases, flipped))
    values = values * (1.0 / (TILE * KT) ** 0.5)
    return values.reshape(NTR, KT, TILE, TILE).astype(jnp.bfloat16)


def place_ends(drawn, rng, smallest, high):
    index_at = [jax.random.randint(jax.random.fold_in(rng, axis), (), 0, length) for axis, length in enumerate(drawn.shape)]
    widest = drawn.shape.index(max(drawn.shape))
    neighbour = index_at[:widest] + [(index_at[widest] + 1) % drawn.shape[widest]] + index_at[widest + 1:]
    return drawn.at[tuple(index_at)].set(smallest).at[tuple(neighbour)].set(high)


def shard_levels(rng, shape, pieces, least, high):
    factor_of, own = 1.0, jax.random.fold_in(rng, 6)
    for dim, blocks in pieces:
        steps = jnp.exp(jax.random.uniform(jax.random.fold_in(own, dim), (blocks,), jnp.float32, least / len(pieces), high / len(pieces)))
        factor_of = factor_of * jnp.repeat(steps, shape[dim] // blocks).reshape([-1 if axis == dim else 1 for axis in range(len(shape))])
    return factor_of


def deal_out(key, own, number, rows, count, top, bound, skew):
    order = jax.random.permutation(key, count)
    crowded, usual = shares(count, rows * top, bound, skew, True), shares(count, rows * top, bound, skew, False)
    places = jnp.arange(count)

    def named(lengths, turn):
        used = int((lengths > 0).sum())
        fixed = max(1, used // 4)
        moved = fixed + (places - fixed + turn * (used - fixed)) % max(1, count - fixed)
        return jnp.zeros((count,), jnp.int32).at[order[jnp.where(places < fixed, places, moved)]].set(jnp.asarray(lengths, jnp.int32))

    lengths = jnp.where(number % 4 == 0, named(crowded, number // 4), named(usual, number - number // 4 - 1))
    mixed = jax.random.permutation(jax.random.fold_in(own, 3), count)
    donor, sink = mixed[0:count // 2 * 2:2], mixed[1:count // 2 * 2:2]
    room = jnp.minimum(lengths[donor] - 1, bound - lengths[sink]) // 2
    room = jnp.where((donor == order[0]) | (sink == order[0]) | (lengths[sink] == 0), 0, jnp.maximum(room, 0))
    moved = jax.random.randint(jax.random.fold_in(own, 4), (count // 2,), 0, 1 << 20) % (room + 1)
    lengths = lengths.at[donor].add(-moved).at[sink].add(moved)
    labels = jnp.searchsorted(jnp.cumsum(lengths), jnp.arange(rows * top), side="right").astype(jnp.int32)
    table = labels.reshape(top, rows).T
    table = table[jax.random.permutation(jax.random.fold_in(own, 1), rows)]
    turn = jax.random.randint(jax.random.fold_in(own, 2), (rows, 1), 0, top)
    return jnp.take_along_axis(table, (jnp.arange(top)[None, :] + turn) % top, axis=1)


def shares(count, total, limit, skew, full):
    loads = [(1 << 20) // math.isqrt(rank ** skew) + 1 for rank in range(1, count + 1)]
    largest = limit if full else min(limit, max(-(-total // count), total * loads[0] // sum(loads)))
    least = 1 if total - largest >= count - 1 else 0
    holding, spare = [largest] + [least] * (count - 1), total - largest - least * (count - 1)
    while spare > 0:
        candidates = [i for i in range(1, count) if holding[i] < largest] or [i for i in range(1, count) if holding[i] < limit]
        mass, budget = sum([loads[i] for i in candidates]), spare
        for i in candidates:
            more = min(limit - holding[i], max(1, budget * loads[i] // mass), spare)
            holding[i] = holding[i] + more
            spare = spare - more
    return np.array(holding)


def centred(stream_key, dims, spread, most, cuts=(), kind=jnp.bfloat16):
    entries = jax.random.normal(stream_key, dims, jnp.float32) * spread
    if len(cuts) > 0:
        entries = shard_levels(stream_key, dims, cuts, -0.22, 0.18) * entries
    return jnp.clip(entries, min=-most, max=most).astype(kind)


def setup_inputs(seed: int = 0) -> dict:
    seeds = jax.random.split(jax.random.key(seed), 7)
    orbitals = centred(seeds[0], (NGRID, NORB), 0.15, 1.1953125, ((0, 16), (1, 8)))
    point_owner_keys = jax.random.split(jax.random.fold_in(seeds[1], 1), NPTS // P_DEV)
    point_owner_turns = jax.random.permutation(jax.random.fold_in(seeds[1], 3), NPTS // P_DEV)
    point_owner = jax.vmap(lambda own, number: deal_out(jax.random.fold_in(seeds[1], 2), own, number, P_DEV, N_GRID, 1, CAP, 2))(point_owner_keys, point_owner_turns).reshape((NPTS, 1))
    point_row = place_ends(jax.random.randint(seeds[2], (NPTS,), 0, GRID_DEV), jax.random.fold_in(seeds[2], 1), 0, GRID_DEV - 1).astype(jnp.int32)
    density_tiles = draw_density_tiles(jax.random.fold_in(seeds[6], 71), 0)
    tile_columns = draw_tile_columns(jax.random.fold_in(seeds[6], 71), 0)
    tile_counts = draw_tile_counts(jax.random.fold_in(seeds[6], 71), 0)
    return {"orbitals": orbitals, "point_owner": point_owner, "point_row": point_row, "density_tiles": density_tiles, "tile_columns": tile_columns, "tile_counts": tile_counts}


def screening(first, second):
    fx = (first % 16).astype(jnp.float32)
    fy = (first // 16 % 16).astype(jnp.float32)
    fz = (first // 256).astype(jnp.float32)
    sx = (second % 16).astype(jnp.float32)
    sy = (second // 16 % 16).astype(jnp.float32)
    sz = (second // 256).astype(jnp.float32)
    dist = (fx[:, None] - sx[None, :]) ** 2 + (fy[:, None] - sy[None, :]) ** 2 + (fz[:, None] - sz[None, :]) ** 2
    return 1.0 / jnp.sqrt(dist + 1.0)

def reference(orbitals, point_owner, point_row, density_tiles, tile_columns, tile_counts):
    index = (point_owner[:, 0] * GRID_DEV + point_row).astype(jnp.int32)
    points = jnp.take(orbitals, index, axis=0)
    tile_rows = NORB // TILE
    blocks = points.reshape(NPTS, tile_rows, TILE)
    valid = (jnp.arange(KT)[None, :] < tile_counts[:, None]).astype(jnp.bfloat16)

    def one_row(args):
        tiles_row, cols_row, valid_row = args
        chosen = jnp.take(blocks, cols_row, axis=1) * valid_row[None, :, None]
        return jnp.einsum('kab,pkb->ap', tiles_row.astype(jnp.float32), chosen.astype(jnp.float32))
    y_full = lax.map(one_row, (density_tiles, tile_columns, valid))
    y_t = y_full.reshape(NORB, NPTS).astype(jnp.bfloat16)
    pair_t = jnp.dot(points, y_t, preferred_element_type=jnp.float32)
    kernel = screening(index, index)
    screened = (pair_t * kernel).astype(jnp.bfloat16)
    result = jnp.dot(screened.T, points, preferred_element_type=jnp.float32)
    return result.astype(jnp.bfloat16)
```

```python
import functools

import jax
import jax.numpy as jnp
from jax import lax
from jax.experimental import pallas as pl
from jax.experimental.pallas import tpu as pltpu
from jax.sharding import PartitionSpec as P

MESH = pl.DeviceIdType.MESH
F32 = jnp.float32
BF16 = jnp.bfloat16
NCH = 4
BLK = 256
COLS = 1536
TILE = 512
CAP = 32
NSEM = 160


def nt(a, b):
    return lax.dot_general(a, b, (((1,), (1,)), ((), ())), preferred_element_type=F32)


def nn(a, b):
    return lax.dot_general(a, b, (((1,), (0,)), ((), ())), preferred_element_type=F32)


def kernel(
    owner_ref, row_ref, cols_ref, counts_ref, orb_hbm, tiles_hbm, out_ref,
    orb, tiles, onehot, slots_out, slots_in, xn, ev0, ev1, ev2, ev3, yg,
    pch, crecv, ysend, yrecv, sfull, rpart, fsend, frecv, ffwd, fsum, pos,
    ss, rs, ls,
):
    every = (ev0, ev1, ev2, ev3)
    rows = BLK // NCH
    half = rows // 2
    g = lax.axis_index("grid")
    b = lax.axis_index("band")
    z, x, y, c = g // 4, g % 4, b // 2, b % 2
    o = 1 - c

    def grid_of(zz, xx):
        return (((zz + 4) % 4) * 4 + (xx + 4) % 4, b)

    def y_of(yy):
        return (g, ((yy + 4) % 4) * 2 + c)

    core_peer = (g, y * 2 + o)
    up = lambda v, d: (v + d + 4) % 4

    counter = [0]
    open_sends = []

    def remote(src, dst, to):
        k = counter[0]
        counter[0] += 1
        return pltpu.make_async_remote_copy(
            src_ref=src, dst_ref=dst, send_sem=ss.at[k], recv_sem=rs.at[k],
            device_id=to, device_id_type=MESH,
        )

    def send(src, dst, to):
        copy = remote(src, dst, to)
        copy.start()
        open_sends.append(copy)
        return copy

    bar = pltpu.get_barrier_semaphore()
    offsets = [(dz, dx) for dz in (2, 1, 3, 0) for dx in (2, 1, 3, 0) if (dz, dx) != (0, 0)]
    for dz, dx in offsets:
        pl.semaphore_signal(bar, inc=1, device_id=grid_of(z + dz, x + dx), device_id_type=MESH)
    for dy in (1, 2, 3):
        pl.semaphore_signal(bar, inc=1, device_id=y_of(y + dy), device_id_type=MESH)
    pl.semaphore_signal(bar, inc=1, device_id=core_peer, device_id_type=MESH)

    load_orb = pltpu.make_async_copy(orb_hbm, orb, ls.at[0])
    load_orb.start()
    load_tiles = pltpu.make_async_copy(tiles_hbm, tiles, ls.at[1])
    load_tiles.start()

    owner = owner_ref[...]
    rowid = row_ref[...]
    holder = (owner == g).astype(F32)
    p0 = lax.broadcasted_iota(jnp.int32, (BLK, BLK), 0)
    p1 = lax.broadcasted_iota(jnp.int32, (BLK, BLK), 1)
    before = (p0 < p1).astype(BF16)
    ahead = nn(holder.astype(BF16), before)
    rowf = rowid.astype(F32)
    slot_id = lax.broadcasted_iota(jnp.int32, (CAP, BLK), 0).astype(F32)
    grid_row = lax.broadcasted_iota(jnp.int32, (CAP, 1024), 1).astype(F32)
    for i in range(16):
        picked = (ahead[i:i + 1, :] == slot_id) & (holder[i:i + 1, :] > 0.5)
        index = jnp.sum(jnp.where(picked, rowf[i:i + 1, :], 0.0), axis=1, keepdims=True)
        onehot[i * CAP:(i + 1) * CAP, :] = (grid_row == index).astype(F32).astype(BF16)

    index = owner * 1024 + rowid
    pos[0] = (index % 16).astype(F32)
    pos[1] = (index // 16 % 16).astype(F32)
    pos[2] = (index // 256).astype(F32)

    load_orb.wait()
    for q in range(4):
        part = slice(q * 128, (q + 1) * 128)
        slots_out[part, :] = nn(onehot[part, :], orb[...]).astype(BF16)

    pl.semaphore_wait(bar, 19)

    a_copies = []
    mine = pl.ds(pl.multiple_of(g * CAP, CAP), CAP)
    for dz, dx in offsets:
        to = grid_of(z + dz, x + dx)
        src = pl.ds(pl.multiple_of(to[0] * CAP, CAP), CAP)
        a_copies.append(send(slots_out.at[src], slots_in.at[mine], to))
    slots_in[mine, :] = slots_out[mine, :]

    own_row = owner_ref[pl.ds(g, 1), :].astype(F32)
    own_col = jnp.sum(jnp.where(p0 == p1, own_row, 0.0), axis=1, keepdims=True)
    rank = jnp.sum(
        jnp.where((own_row == own_col) & (p1 < p0), 1.0, 0.0), axis=1, keepdims=True
    )
    flat = own_col * CAP + rank
    slot_no = lax.broadcasted_iota(jnp.int32, (BLK, 16 * CAP), 1).astype(F32)
    unpermute = (slot_no == flat).astype(F32).astype(BF16)
    for copy in a_copies:
        copy.wait_recv()
    points = nn(unpermute, slots_in[...]).astype(BF16)
    xn[x] = points
    for k in range(NCH):
        for t in range(3):
            every[k][b * 3 + t] = points[k * rows:(k + 1) * rows, t * TILE:(t + 1) * TILE]

    up1, dn1, far = up(y, 1), up(y, -1), up(y, 2)
    st = {}

    def tri(yy, cc):
        return pl.ds((yy * 2 + cc) * 3, 3)

    def b_send(k):
        src = every[k].at[tri(y, c)]
        st["bp", k] = send(src, src, y_of(y + 1))
        st["bm", k] = send(src, src, y_of(y - 1))
        st["bc", k] = [send(src, src, core_peer)]

    def b_fwd(k):
        h0, h1 = pl.ds(0, half), pl.ds(half, half)
        st["bp", k].wait_recv()
        src = every[k].at[tri(dn1, c), h0]
        st["bfp", k] = send(src, src, y_of(y + 1))
        src = every[k].at[tri(dn1, c)]
        st["bc", k].append(send(src, src, core_peer))
        st["bm", k].wait_recv()
        src = every[k].at[tri(up1, c), h1]
        st["bfm", k] = send(src, src, y_of(y - 1))
        src = every[k].at[tri(up1, c)]
        st["bc", k].append(send(src, src, core_peer))

    def b_fin(k):
        st["bfp", k].wait_recv()
        st["bfm", k].wait_recv()
        src = every[k].at[tri(far, c)]
        st["bc", k].append(send(src, src, core_peer))

    def y_stage(k):
        for copy in st["bc", k]:
            copy.wait_recv()
        if k == 0:
            load_tiles.wait()
        for r in range(3):
            acc = jnp.zeros((rows, TILE), F32)
            count = counts_ref[r]
            for s in range(6):
                block = every[k][cols_ref[r, s]]
                if s > 0:
                    keep = (count > s).astype(F32)
                    block = block * keep.astype(BF16)
                acc = acc + nt(block, tiles[r * 6 + s])
            yg[z, k * rows:(k + 1) * rows, r * TILE:(r + 1) * TILE] = acc.astype(BF16)

    def c_send():
        src = xn.at[x]
        st["cp"] = send(src, src, grid_of(z, x + 1))
        st["cm"] = send(src, src, grid_of(z, x - 1))

    def c_fwd():
        st["cp"].wait_recv()
        src = xn.at[up(x, -1), pl.ds(0, 128)]
        st["cfp"] = send(src, src, grid_of(z, x + 1))
        st["cm"].wait_recv()
        src = xn.at[up(x, 1), pl.ds(128, 128)]
        st["cfm"] = send(src, src, grid_of(z, x - 1))

    def c_fin():
        st["cfp"].wait_recv()
        st["cfm"].wait_recv()

    def d_send(k):
        src = yg.at[z, pl.ds(k * rows, rows)]
        st["dp", k] = send(src, src, grid_of(z + 1, x))
        st["dm", k] = send(src, src, grid_of(z - 1, x))

    def d_fwd(k):
        st["dp", k].wait_recv()
        src = yg.at[up(z, -1), pl.ds(k * rows, half)]
        st["dfp", k] = send(src, src, grid_of(z + 1, x))
        st["dm", k].wait_recv()
        src = yg.at[up(z, 1), pl.ds(k * rows + half, half)]
        st["dfm", k] = send(src, src, grid_of(z - 1, x))

    def pair(k):
        st["dfp", k].wait_recv()
        st["dfm", k].wait_recv()
        lhs = yg[:, k * rows:(k + 1) * rows, :].reshape(4 * rows, COLS)
        for h in range(2):
            rhs = xn[2 * h:2 * h + 2].reshape(2 * BLK, COLS)
            pch[k, h] = nt(lhs, rhs)
        st["e1", k] = send(pch.at[k, o], crecv.at[k], core_peer)

    def e2(k):
        st["e1", k].wait_recv()
        total = pch[k, c] + crecv[k]
        pch[k, c] = total
        ysend[k] = total.astype(BF16).reshape(4, rows, TILE)
        for d in (2, 1, 3):
            st["e2", k, d] = send(
                ysend.at[k, up(y, d)], yrecv.at[k, d - 1], y_of(y + d)
            )

    def e3(k):
        mine = pl.ds(pl.multiple_of(y * rows, rows), rows)
        total = pch[k, c, mine, :]
        for d in (1, 2, 3):
            st["e2", k, d].wait_recv()
            total = total + yrecv[k, d - 1].astype(F32)
        eye0 = lax.broadcasted_iota(jnp.int32, (rows, BLK), 0) + k * rows
        eye1 = lax.broadcasted_iota(jnp.int32, (rows, BLK), 1)
        eye = eye0 == eye1
        sides = []
        mu_at = [
            jnp.sum(jnp.where(eye, pos[a, pl.ds(y * 4 + x, 1), :], 0.0), axis=1, keepdims=True)
            for a in range(3)
        ]
        for h in range(2):
            dist = jnp.ones((rows, BLK), F32)
            for a in range(3):
                delta = mu_at[a] - pos[a, pl.ds(z * 4 + 2 * c + h, 1), :]
                dist = dist + delta * delta
            sides.append(lax.rsqrt(dist))
        kern = jnp.concatenate(sides, axis=1)
        sfull[k, c, y] = (total * kern).astype(BF16)
        src = sfull.at[k, c, y]
        for d in (2, 1, 3):
            st["e3", k, d] = send(src, src, y_of(y + d))

    def e4(k):
        for d in (1, 2, 3):
            st["e3", k, d].wait_recv()
        src = sfull.at[k, c]
        st["e4", k] = send(src, src, core_peer)

    def res(k):
        st["e4", k].wait_recv()
        total = nn(sfull[k, 0].reshape(4 * rows, 2 * BLK), xn[0:2].reshape(2 * BLK, COLS))
        total = total + nn(sfull[k, 1].reshape(4 * rows, 2 * BLK), xn[2:4].reshape(2 * BLK, COLS))
        rpart[k] = total.reshape(4, rows, COLS)
        fsend[k] = total.astype(BF16).reshape(4, rows, COLS)
        far_z, up_z, dn_z = up(z, 2), up(z, 1), up(z, -1)
        lo, hi = pl.ds(0, half), pl.ds(half, half)
        st["fp", k] = send(fsend.at[k, far_z, lo], ffwd.at[k, 0], grid_of(z + 1, x))
        st["fm", k] = send(fsend.at[k, far_z, hi], ffwd.at[k, 1], grid_of(z - 1, x))
        st["fdp", k] = send(fsend.at[k, up_z, hi], frecv.at[k, 0], grid_of(z + 1, x))
        st["fdm", k] = send(fsend.at[k, dn_z, lo], frecv.at[k, 1], grid_of(z - 1, x))

    def f_fwd(k):
        up_z, dn_z = up(z, 1), up(z, -1)
        st["fp", k].wait_recv()
        fsum[k, 0] = (rpart[k, up_z, 0:half, :] + ffwd[k, 0].astype(F32)).astype(BF16)
        st["fsp", k] = send(fsum.at[k, 0], frecv.at[k, 2], grid_of(z + 1, x))
        st["fm", k].wait_recv()
        fsum[k, 1] = (rpart[k, dn_z, half:rows, :] + ffwd[k, 1].astype(F32)).astype(BF16)
        st["fsm", k] = send(fsum.at[k, 1], frecv.at[k, 3], grid_of(z - 1, x))

    def f_fin(k):
        for name in ("fdp", "fdm", "fsp", "fsm"):
            st[name, k].wait_recv()
        lo = rpart[k, z, 0:half, :] + frecv[k, 2].astype(F32) + frecv[k, 1].astype(F32)
        hi = rpart[k, z, half:rows, :] + frecv[k, 0].astype(F32) + frecv[k, 3].astype(F32)
        out_ref[k * rows:k * rows + half, :] = lo.astype(BF16)
        out_ref[k * rows + half:(k + 1) * rows, :] = hi.astype(BF16)

    b_send(0)
    c_send()
    for t in range(1, NCH + 8):
        def at(offset):
            k = t - offset
            return k if 0 <= k < NCH else None

        if t < NCH:
            b_send(t)
        if at(1) is not None:
            b_fwd(t - 1)
            b_fin(t - 1)
            y_stage(t - 1)
            d_send(t - 1)
        if t == 2:
            c_fwd()
        if at(2) is not None:
            d_fwd(t - 2)
        if t == 3:
            c_fin()
        if at(5) is not None:
            e3(t - 5)
        if at(6) is not None:
            e4(t - 6)
        if at(4) is not None:
            e2(t - 4)
        if at(3) is not None:
            pair(t - 3)
        if at(6) is not None:
            res(t - 6)
        if at(7) is not None:
            f_fwd(t - 7)
    for k in range(NCH):
        f_fin(k)
    for copy in open_sends:
        copy.wait_send()


def local(orbitals, point_owner, point_row, density_tiles, tile_columns, tile_counts):
    rows = BLK // NCH
    half = rows // 2
    vmem = pl.BlockSpec(memory_space=pltpu.VMEM)
    smem = pl.BlockSpec(memory_space=pltpu.SMEM)
    hbm = pl.BlockSpec(memory_space=pl.ANY)
    return pl.pallas_call(
        kernel,
        name="exchange",
        out_shape=jax.ShapeDtypeStruct((BLK, COLS), BF16),
        in_specs=[vmem, vmem, smem, smem, hbm, hbm],
        out_specs=vmem,
        scratch_shapes=[
            pltpu.VMEM((1024, COLS), BF16),
            pltpu.VMEM((18, TILE, TILE), BF16),
            pltpu.VMEM((512, 1024), BF16),
            pltpu.VMEM((512, COLS), BF16),
            pltpu.VMEM((512, COLS), BF16),
            pltpu.VMEM((4, BLK, COLS), BF16),
            pltpu.VMEM((24, rows, TILE), BF16),
            pltpu.VMEM((24, rows, TILE), BF16),
            pltpu.VMEM((24, rows, TILE), BF16),
            pltpu.VMEM((24, rows, TILE), BF16),
            pltpu.VMEM((4, BLK, COLS), BF16),
            pltpu.VMEM((NCH, 2, 4 * rows, TILE), F32),
            pltpu.VMEM((NCH, 4 * rows, TILE), F32),
            pltpu.VMEM((NCH, 4, rows, TILE), BF16),
            pltpu.VMEM((NCH, 3, rows, TILE), BF16),
            pltpu.VMEM((NCH, 2, 4, rows, TILE), BF16),
            pltpu.VMEM((NCH, 4, rows, COLS), F32),
            pltpu.VMEM((NCH, 4, rows, COLS), BF16),
            pltpu.VMEM((NCH, 4, half, COLS), BF16),
            pltpu.VMEM((NCH, 2, half, COLS), BF16),
            pltpu.VMEM((NCH, 2, half, COLS), BF16),
            pltpu.VMEM((3, 16, BLK), F32),
            pltpu.SemaphoreType.DMA((NSEM,)),
            pltpu.SemaphoreType.DMA((NSEM,)),
            pltpu.SemaphoreType.DMA((2,)),
        ],
        compiler_params=pltpu.CompilerParams(
            collective_id=0, has_side_effects=True, vmem_limit_bytes=60 * 2**20
        ),
        cost_estimate=pl.CostEstimate(
            flops=12_000_000_000, bytes_accessed=14_000_000, transcendentals=0
        ),
    )(
        point_owner.reshape(16, BLK),
        point_row.reshape(16, BLK),
        tile_columns,
        tile_counts,
        orbitals,
        density_tiles.reshape(18, TILE, TILE),
    )


def solution(mesh):
    in_specs = (
        P("grid", "band"),
        P(),
        P(),
        P("band", None, None, None),
        P("band", None),
        P("band"),
    )
    return jax.shard_map(
        local, mesh=mesh, in_specs=in_specs, out_specs=P("grid", "band"), check_vma=False
    )
```

```python
import functools

import jax
import jax.numpy as jnp
from jax import lax
from jax.experimental import pallas as pl
from jax.experimental.pallas import tpu as pltpu
from jax.sharding import PartitionSpec as P

MESH = pl.DeviceIdType.MESH
F32 = jnp.float32
BF16 = jnp.bfloat16
NCH = 4
BLK = 256
COLS = 1536
TILE = 512
CAP = 32
NSEM = 192


def nt(a, b):
    return lax.dot_general(a, b, (((1,), (1,)), ((), ())), preferred_element_type=F32)


def nn(a, b):
    return lax.dot_general(a, b, (((1,), (0,)), ((), ())), preferred_element_type=F32)


def kernel(
    index_ref, cols_ref, counts_ref, orb_hbm, tiles_hbm, out_ref,
    orb, tiles, onehot, slots_out, slots_in, xn, ev0, ev1, ev2, ev3, yg,
    pch, crecv, ysend, yrecv, sfull, rpart, fsend, frecv, ffwd, fsum, pos,
    ss, rs, ls,
):
    every = (ev0, ev1, ev2, ev3)
    rows = BLK // NCH
    half = rows // 2
    g = lax.axis_index("grid")
    b = lax.axis_index("band")
    z, x, y, c = g // 4, g % 4, b // 2, b % 2
    o = 1 - c

    def grid_of(zz, xx):
        return (((zz + 4) % 4) * 4 + (xx + 4) % 4, b)

    def y_of(yy):
        return (g, ((yy + 4) % 4) * 2 + c)

    core_peer = (g, y * 2 + o)
    up = lambda v, d: (v + d + 4) % 4

    place = (z, x)

    def ring(mode, d):
        return grid_of(z + d, x) if mode == 0 else grid_of(z, x + d)

    counter = [0]
    open_sends = []

    def send(src, dst, to):
        k = counter[0]
        counter[0] += 1
        copy = pltpu.make_async_remote_copy(
            src_ref=src, dst_ref=dst, send_sem=ss.at[k], recv_sem=rs.at[k],
            device_id=to, device_id_type=MESH,
        )
        copy.start()
        open_sends.append(copy)
        return copy

    bar = pltpu.get_barrier_semaphore()
    for dz in (2, 1, 3, 0):
        for dx in (2, 1, 3, 0):
            if (dz, dx) != (0, 0):
                pl.semaphore_signal(
                    bar, inc=1, device_id=grid_of(z + dz, x + dx), device_id_type=MESH
                )
    for dy in (1, 2, 3):
        pl.semaphore_signal(bar, inc=1, device_id=y_of(y + dy), device_id_type=MESH)
    pl.semaphore_signal(bar, inc=1, device_id=core_peer, device_id_type=MESH)

    load_orb = pltpu.make_async_copy(orb_hbm, orb, ls.at[0])
    load_orb.start()
    load_tiles = pltpu.make_async_copy(tiles_hbm, tiles, ls.at[1])
    load_tiles.start()

    index = index_ref[...]
    owner = index // 1024
    rowf = (index % 1024).astype(F32)
    holder = (owner == g).astype(F32)
    p0 = lax.broadcasted_iota(jnp.int32, (BLK, BLK), 0)
    p1 = lax.broadcasted_iota(jnp.int32, (BLK, BLK), 1)
    before = (p0 < p1).astype(BF16)
    ahead = nn(holder.astype(BF16), before)
    slot_id = lax.broadcasted_iota(jnp.int32, (CAP, BLK), 0).astype(F32)
    grid_row = lax.broadcasted_iota(jnp.int32, (CAP, 1024), 1).astype(F32)
    for i in range(16):
        picked = (ahead[i:i + 1, :] == slot_id) & (holder[i:i + 1, :] > 0.5)
        wanted = jnp.sum(jnp.where(picked, rowf[i:i + 1, :], 0.0), axis=1, keepdims=True)
        onehot[i * CAP:(i + 1) * CAP, :] = (grid_row == wanted).astype(F32).astype(BF16)

    load_orb.wait()
    a_copies = []
    mine = pl.ds(pl.multiple_of(g * CAP, CAP), CAP)
    for q in range(3):
        piece = []
        for dz in (2, 1, 3, 0):
            part = pl.ds(pl.multiple_of(up(z, dz) * 128, 128), 128)
            slots_out[q, part, :] = nn(
                onehot[part, :], orb[:, q * TILE:(q + 1) * TILE]
            ).astype(BF16)
            if q == 0 and dz == 2:
                pl.semaphore_wait(bar, 19)
            for dx in (2, 1, 3, 0):
                if (dz, dx) == (0, 0):
                    continue
                to = grid_of(z + dz, x + dx)
                src = pl.ds(pl.multiple_of(to[0] * CAP, CAP), CAP)
                piece.append(send(slots_out.at[q, src], slots_in.at[q, mine], to))
        slots_in[q, mine, :] = slots_out[q, mine, :]
        a_copies.append(piece)

    pos[0] = (index % 16).astype(F32)
    pos[1] = (index // 16 % 16).astype(F32)
    pos[2] = (index // 256).astype(F32)
    own_row = (index_ref[pl.ds(g, 1), :] // 1024).astype(F32)
    own_col = jnp.sum(jnp.where(p0 == p1, own_row, 0.0), axis=1, keepdims=True)
    rank = jnp.sum(
        jnp.where((own_row == own_col) & (p1 < p0), 1.0, 0.0), axis=1, keepdims=True
    )
    flat = own_col * CAP + rank
    slot_no = lax.broadcasted_iota(jnp.int32, (BLK, 16 * CAP), 1).astype(F32)
    unpermute = (slot_no == flat).astype(F32).astype(BF16)

    st = {}

    def a_fin(q):
        for copy in a_copies[q]:
            copy.wait_recv()
        points = nn(unpermute, slots_in[q]).astype(BF16)
        xn[0, q, x] = points
        xn[1, q, z] = points
        for k in range(NCH):
            every[k][c * 12 + q * 4 + y] = points[k * rows:(k + 1) * rows, :]

    def b_send(q, k):
        src = every[k].at[c * 12 + q * 4 + y]
        st["b", q, k] = [send(src, src, y_of(y + d)) for d in (2, 1, 3)]

    def b_core(q, k):
        for copy in st["b", q, k]:
            copy.wait_recv()
        src = every[k].at[pl.ds(c * 12 + q * 4, 4)]
        st["bc", q, k] = send(src, src, core_peer)

    def y_stage(k):
        for q in range(3):
            st["bc", q, k].wait_recv()
        if k == 0:
            load_tiles.wait()
        for r in range(3):
            acc = jnp.zeros((rows, TILE), F32)
            count = counts_ref[r]
            for s in range(6):
                col = cols_ref[r, s]
                block = every[k][(col // 3 % 2) * 12 + (col % 3) * 4 + col // 6]
                if s > 0:
                    keep = (count > s).astype(F32)
                    block = block * keep.astype(BF16)
                acc = acc + nt(block, tiles[r * 6 + s])
            yg[place_of(k), k * rows:(k + 1) * rows, r * TILE:(r + 1) * TILE] = acc.astype(BF16)

    def place_of(k):
        return place[k % 2]

    def c_send(q):
        for mode in range(2):
            v = place[1 - mode]
            src = xn.at[mode, q, v]
            st["c", q, mode] = [send(src, src, ring(1 - mode, d)) for d in (1, -1)]

    def c_fwd(q):
        for mode in range(2):
            v = place[1 - mode]
            plus, minus = st["c", q, mode]
            plus.wait_recv()
            src = xn.at[mode, q, up(v, -1), pl.ds(0, 128)]
            ahead_copy = send(src, src, ring(1 - mode, 1))
            minus.wait_recv()
            src = xn.at[mode, q, up(v, 1), pl.ds(128, 128)]
            st["cf", q, mode] = (ahead_copy, send(src, src, ring(1 - mode, -1)))

    def c_fin(q):
        for mode in range(2):
            for copy in st["cf", q, mode]:
                copy.wait_recv()

    def d_send(k):
        src = yg.at[place_of(k), pl.ds(k * rows, rows)]
        st["dp", k] = send(src, src, ring(k % 2, 1))
        st["dm", k] = send(src, src, ring(k % 2, -1))

    def d_fwd(k):
        st["dp", k].wait_recv()
        src = yg.at[up(place_of(k), -1), pl.ds(k * rows, half)]
        st["dfp", k] = send(src, src, ring(k % 2, 1))
        st["dm", k].wait_recv()
        src = yg.at[up(place_of(k), 1), pl.ds(k * rows + half, half)]
        st["dfm", k] = send(src, src, ring(k % 2, -1))

    def pair(k):
        st["dfp", k].wait_recv()
        st["dfm", k].wait_recv()
        mode = k % 2
        for h in (o, c):
            total = None
            for q in range(3):
                lhs = yg[:, k * rows:(k + 1) * rows, q * TILE:(q + 1) * TILE]
                rhs = xn[mode, q, pl.ds(2 * h, 2)]
                term = nt(lhs.reshape(4 * rows, TILE), rhs.reshape(2 * BLK, TILE))
                total = term if total is None else total + term
            pch[k, h] = total
            if h is o:
                st["e1", k] = send(pch.at[k, o], crecv.at[k], core_peer)

    def e2(k):
        st["e1", k].wait_recv()
        total = pch[k, c] + crecv[k]
        pch[k, c] = total
        ysend[k] = total.astype(BF16).reshape(4, rows, TILE)
        for d in (2, 1, 3):
            st["e2", k, d] = send(
                ysend.at[k, up(y, d)], yrecv.at[k, d - 1], y_of(y + d)
            )

    def e3(k):
        part = pl.ds(pl.multiple_of(y * rows, rows), rows)
        total = pch[k, c, part, :]
        for d in (1, 2, 3):
            st["e2", k, d].wait_recv()
            total = total + yrecv[k, d - 1].astype(F32)
        eye0 = lax.broadcasted_iota(jnp.int32, (rows, BLK), 0) + k * rows
        eye1 = lax.broadcasted_iota(jnp.int32, (rows, BLK), 1)
        eye = eye0 == eye1
        mu_block = y * 4 + x if k % 2 == 0 else z * 4 + y
        sides = []
        mu_at = [
            jnp.sum(jnp.where(eye, pos[a, pl.ds(mu_block, 1), :], 0.0), axis=1, keepdims=True)
            for a in range(3)
        ]
        for h in range(2):
            nu_block = z * 4 + 2 * c + h if k % 2 == 0 else (2 * c + h) * 4 + x
            dist = jnp.ones((rows, BLK), F32)
            for a in range(3):
                delta = mu_at[a] - pos[a, pl.ds(nu_block, 1), :]
                dist = dist + delta * delta
            sides.append(lax.rsqrt(dist))
        kern = jnp.concatenate(sides, axis=1)
        sfull[k, c, y] = (total * kern).astype(BF16)
        src = sfull.at[k, c, y]
        for d in (2, 1, 3):
            st["e3", k, d] = send(src, src, y_of(y + d))

    def e4(k):
        for d in (1, 2, 3):
            st["e3", k, d].wait_recv()
        src = sfull.at[k, c]
        st["e4", k] = send(src, src, core_peer)

    def res(k):
        st["e4", k].wait_recv()
        mode = k % 2
        lhs = [sfull[k, h].reshape(4 * rows, 2 * BLK) for h in range(2)]
        for q in range(3):
            total = nn(lhs[0], xn[mode, q, 0:2].reshape(2 * BLK, TILE))
            total = total + nn(lhs[1], xn[mode, q, 2:4].reshape(2 * BLK, TILE))
            cut = slice(q * TILE, (q + 1) * TILE)
            rpart[k, :, :, cut] = total.reshape(4, rows, TILE)
            fsend[k, :, :, cut] = total.astype(BF16).reshape(4, rows, TILE)
        v = place_of(k)
        far_v, up_v, dn_v = up(v, 2), up(v, 1), up(v, -1)
        lo, hi = pl.ds(0, half), pl.ds(half, half)
        st["fp", k] = send(fsend.at[k, far_v, lo], ffwd.at[k, 0], ring(mode, 1))
        st["fm", k] = send(fsend.at[k, far_v, hi], ffwd.at[k, 1], ring(mode, -1))
        st["fdp", k] = send(fsend.at[k, up_v, hi], frecv.at[k, 0], ring(mode, 1))
        st["fdm", k] = send(fsend.at[k, dn_v, lo], frecv.at[k, 1], ring(mode, -1))

    def f_fwd(k):
        up_v, dn_v = up(place_of(k), 1), up(place_of(k), -1)
        st["fp", k].wait_recv()
        fsum[k, 0] = (rpart[k, up_v, 0:half, :] + ffwd[k, 0].astype(F32)).astype(BF16)
        st["fsp", k] = send(fsum.at[k, 0], frecv.at[k, 2], ring(k % 2, 1))
        st["fm", k].wait_recv()
        fsum[k, 1] = (rpart[k, dn_v, half:rows, :] + ffwd[k, 1].astype(F32)).astype(BF16)
        st["fsm", k] = send(fsum.at[k, 1], frecv.at[k, 3], ring(k % 2, -1))

    def f_fin(k):
        v = place_of(k)
        for name in ("fdp", "fdm", "fsp", "fsm"):
            st[name, k].wait_recv()
        lo = rpart[k, v, 0:half, :] + frecv[k, 2].astype(F32) + frecv[k, 1].astype(F32)
        hi = rpart[k, v, half:rows, :] + frecv[k, 0].astype(F32) + frecv[k, 3].astype(F32)
        out_ref[k * rows:k * rows + half, :] = lo.astype(BF16)
        out_ref[k * rows + half:(k + 1) * rows, :] = hi.astype(BF16)

    steps = []
    for q in range(3):
        steps += [(a_fin, q)] + [(b_send, q, k) for k in range(NCH)] + [(c_send, q)]
    steps += [(b_core, 0, k) for k in range(NCH)] + [(b_core, 1, k) for k in range(NCH)]
    steps += [
        (b_core, 2, 0), (c_fwd, 0), (y_stage, 0), (d_send, 0),
        (b_core, 2, 1), (y_stage, 1), (d_send, 1),
        (c_fwd, 1), (b_core, 2, 2), (y_stage, 2), (d_send, 2),
        (b_core, 2, 3), (y_stage, 3), (d_send, 3),
        (c_fwd, 2), (d_fwd, 0), (d_fwd, 1), (c_fin, 0), (c_fin, 1), (c_fin, 2),
        (pair, 0), (pair, 1), (d_fwd, 2), (e2, 0), (e2, 1), (d_fwd, 3),
        (e3, 0), (pair, 2), (e3, 1), (pair, 3),
        (e4, 0), (e2, 2), (e4, 1), (e2, 3),
        (res, 0), (e3, 2), (res, 1), (e3, 3), (e4, 2), (e4, 3),
        (f_fwd, 0), (f_fwd, 1), (res, 2), (res, 3), (f_fwd, 2), (f_fwd, 3),
    ]
    steps += [(f_fin, k) for k in range(NCH)]
    for stage, *at in steps:
        stage(*at)
    for copy in open_sends:
        copy.wait_send()


def local(orbitals, point_owner, point_row, density_tiles, tile_columns, tile_counts):
    rows = BLK // NCH
    half = rows // 2
    vmem = pl.BlockSpec(memory_space=pltpu.VMEM)
    smem = pl.BlockSpec(memory_space=pltpu.SMEM)
    hbm = pl.BlockSpec(memory_space=pl.ANY)
    return pl.pallas_call(
        kernel,
        name="exchange",
        out_shape=jax.ShapeDtypeStruct((BLK, COLS), BF16),
        in_specs=[vmem, smem, smem, hbm, hbm],
        out_specs=vmem,
        scratch_shapes=[
            pltpu.VMEM((1024, COLS), BF16),
            pltpu.VMEM((18, TILE, TILE), BF16),
            pltpu.VMEM((512, 1024), BF16),
            pltpu.VMEM((3, 512, TILE), BF16),
            pltpu.VMEM((3, 512, TILE), BF16),
            pltpu.VMEM((2, 3, 4, BLK, TILE), BF16),
            pltpu.VMEM((24, rows, TILE), BF16),
            pltpu.VMEM((24, rows, TILE), BF16),
            pltpu.VMEM((24, rows, TILE), BF16),
            pltpu.VMEM((24, rows, TILE), BF16),
            pltpu.VMEM((4, BLK, COLS), BF16),
            pltpu.VMEM((NCH, 2, 4 * rows, TILE), F32),
            pltpu.VMEM((NCH, 4 * rows, TILE), F32),
            pltpu.VMEM((NCH, 4, rows, TILE), BF16),
            pltpu.VMEM((NCH, 3, rows, TILE), BF16),
            pltpu.VMEM((NCH, 2, 4, rows, TILE), BF16),
            pltpu.VMEM((NCH, 4, rows, COLS), F32),
            pltpu.VMEM((NCH, 4, rows, COLS), BF16),
            pltpu.VMEM((NCH, 4, half, COLS), BF16),
            pltpu.VMEM((NCH, 2, half, COLS), BF16),
            pltpu.VMEM((NCH, 2, half, COLS), BF16),
            pltpu.VMEM((3, 16, BLK), F32),
            pltpu.SemaphoreType.DMA((NSEM,)),
            pltpu.SemaphoreType.DMA((NSEM,)),
            pltpu.SemaphoreType.DMA((2,)),
        ],
        compiler_params=pltpu.CompilerParams(
            collective_id=0, has_side_effects=True, vmem_limit_bytes=60 * 2**20
        ),
        cost_estimate=pl.CostEstimate(
            flops=12_000_000_000, bytes_accessed=14_000_000, transcendentals=0
        ),
    )(
        (point_owner[:, 0] * 1024 + point_row).reshape(16, BLK),
        tile_columns,
        tile_counts,
        orbitals,
        density_tiles.reshape(18, TILE, TILE),
    )


def solution(mesh):
    in_specs = (
        P("grid", "band"),
        P(),
        P(),
        P("band", None, None, None),
        P("band", None),
        P("band"),
    )
    return jax.shard_map(
        local, mesh=mesh, in_specs=in_specs, out_specs=P("grid", "band"), check_vma=False
    )
```

```python
import functools

import jax
import jax.numpy as jnp
from jax import lax
from jax.experimental import pallas as pl
from jax.experimental.pallas import tpu as pltpu
from jax.sharding import PartitionSpec as P

MESH = pl.DeviceIdType.MESH
F32 = jnp.float32
BF16 = jnp.bfloat16
NCH = 4
BLK = 256
COLS = 1536
TILE = 512
CAP = 32
NSEM = 192
WINDOW = 3


def nt(a, b):
    return lax.dot_general(a, b, (((1,), (1,)), ((), ())), preferred_element_type=F32)


def nn(a, b):
    return lax.dot_general(a, b, (((1,), (0,)), ((), ())), preferred_element_type=F32)


def kernel(
    index_ref, cols_ref, counts_ref, orb_hbm, tiles_hbm, out_ref,
    orb, tiles, onehot, slots_out, slots_in, xn, ev0, ev1, ev2, ev3, yg,
    pch, crecv, ysend, yrecv, sfull, rpart, fsend, frecv, ffwd, fsum, pos,
    ss, rs, ls,
):
    every = (ev0, ev1, ev2, ev3)
    rows = BLK // NCH
    half = rows // 2
    g = lax.axis_index("grid")
    b = lax.axis_index("band")
    z, x, y, c = g // 4, g % 4, b // 2, b % 2
    o = 1 - c

    def grid_of(zz, xx):
        return (((zz + 4) % 4) * 4 + (xx + 4) % 4, b)

    def y_of(yy):
        return (g, ((yy + 4) % 4) * 2 + c)

    core_peer = (g, y * 2 + o)
    up = lambda v, d: (v + d + 4) % 4

    place = (z, x)

    def ring(mode, d):
        return grid_of(z + d, x) if mode == 0 else grid_of(z, x + d)

    counter = [0]
    open_sends = []

    def send(src, dst, to):
        k = counter[0]
        counter[0] += 1
        copy = pltpu.make_async_remote_copy(
            src_ref=src, dst_ref=dst, send_sem=ss.at[k], recv_sem=rs.at[k],
            device_id=to, device_id_type=MESH,
        )
        copy.start()
        open_sends.append(copy)
        return copy

    bar = pltpu.get_barrier_semaphore()
    for dz in (2, 1, 3, 0):
        for dx in (2, 1, 3, 0):
            if (dz, dx) != (0, 0):
                pl.semaphore_signal(
                    bar, inc=1, device_id=grid_of(z + dz, x + dx), device_id_type=MESH
                )
    for dy in (1, 2, 3):
        pl.semaphore_signal(bar, inc=1, device_id=y_of(y + dy), device_id_type=MESH)
    pl.semaphore_signal(bar, inc=1, device_id=core_peer, device_id_type=MESH)

    load_orb = pltpu.make_async_copy(orb_hbm, orb, ls.at[0])
    load_orb.start()
    load_tiles = pltpu.make_async_copy(tiles_hbm, tiles, ls.at[1])
    load_tiles.start()

    index = index_ref[...]
    owner = index // 1024
    rowf = (index % 1024).astype(F32)
    holder = (owner == g).astype(F32)
    p0 = lax.broadcasted_iota(jnp.int32, (BLK, BLK), 0)
    p1 = lax.broadcasted_iota(jnp.int32, (BLK, BLK), 1)
    before = (p0 < p1).astype(BF16)
    ahead = nn(holder.astype(BF16), before)
    slot_id = lax.broadcasted_iota(jnp.int32, (CAP, BLK), 0).astype(F32)
    grid_row = lax.broadcasted_iota(jnp.int32, (CAP, 1024), 1).astype(F32)
    for i in range(16):
        picked = (ahead[i:i + 1, :] == slot_id) & (holder[i:i + 1, :] > 0.5)
        wanted = jnp.sum(jnp.where(picked, rowf[i:i + 1, :], 0.0), axis=1, keepdims=True)
        onehot[i * CAP:(i + 1) * CAP, :] = (grid_row == wanted).astype(F32).astype(BF16)

    load_orb.wait()
    mine = pl.ds(pl.multiple_of(g * CAP, CAP), CAP)
    pieces = [(q, dz) for q in range(3) for dz in (2, 1, 3, 0)]
    a_copies = []

    def a_rows(s):
        q, dz = pieces[s]
        part = pl.ds(pl.multiple_of(up(z, dz) * 128, 128), 128)
        slots_out[q, part, :] = nn(
            onehot[part, :], orb[:, q * TILE:(q + 1) * TILE]
        ).astype(BF16)

    def a_send(s):
        if s >= WINDOW:
            for copy in a_copies[s - WINDOW]:
                copy.wait_send()
                open_sends[:] = [other for other in open_sends if other is not copy]
        q, dz = pieces[s]
        group = []
        for dx in (2, 1, 3, 0):
            if (dz, dx) != (0, 0):
                to = grid_of(z + dz, x + dx)
                src = pl.ds(pl.multiple_of(to[0] * CAP, CAP), CAP)
                group.append(send(slots_out.at[q, src], slots_in.at[q, mine], to))
        a_copies.append(group)

    for s in range(WINDOW):
        a_rows(s)
        if s == 0:
            pl.semaphore_wait(bar, 19)
        a_send(s)
    for s in range(WINDOW, 12):
        a_rows(s)
    for q in range(3):
        slots_in[q, mine, :] = slots_out[q, mine, :]

    pos[0] = (index % 16).astype(F32)
    pos[1] = (index // 16 % 16).astype(F32)
    pos[2] = (index // 256).astype(F32)
    own_row = (index_ref[pl.ds(g, 1), :] // 1024).astype(F32)
    own_col = jnp.sum(jnp.where(p0 == p1, own_row, 0.0), axis=1, keepdims=True)
    rank = jnp.sum(
        jnp.where((own_row == own_col) & (p1 < p0), 1.0, 0.0), axis=1, keepdims=True
    )
    flat = own_col * CAP + rank
    slot_no = lax.broadcasted_iota(jnp.int32, (BLK, 16 * CAP), 1).astype(F32)
    unpermute = (slot_no == flat).astype(F32).astype(BF16)

    st = {}

    def a_fin(q):
        for group in a_copies[4 * q:4 * q + 4]:
            for copy in group:
                copy.wait_recv()
        points = nn(unpermute, slots_in[q]).astype(BF16)
        xn[0, q, x] = points
        xn[1, q, z] = points
        for k in range(NCH):
            every[k][c * 12 + q * 4 + y] = points[k * rows:(k + 1) * rows, :]

    def b_send(q, k):
        src = every[k].at[c * 12 + q * 4 + y]
        st["b", q, k] = [send(src, src, y_of(y + d)) for d in (2, 1, 3)]

    def b_core(q, k):
        for copy in st["b", q, k]:
            copy.wait_recv()
        src = every[k].at[pl.ds(c * 12 + q * 4, 4)]
        st["bc", q, k] = send(src, src, core_peer)

    def y_stage(k):
        for q in range(3):
            st["bc", q, k].wait_recv()
        if k == 0:
            load_tiles.wait()
        for r in range(3):
            acc = jnp.zeros((rows, TILE), F32)
            count = counts_ref[r]
            for s in range(6):
                col = cols_ref[r, s]
                block = every[k][(col // 3 % 2) * 12 + (col % 3) * 4 + col // 6]
                if s > 0:
                    keep = (count > s).astype(F32)
                    block = block * keep.astype(BF16)
                acc = acc + nt(block, tiles[r * 6 + s])
            yg[place_of(k), k * rows:(k + 1) * rows, r * TILE:(r + 1) * TILE] = acc.astype(BF16)

    def place_of(k):
        return place[k % 2]

    def c_send(q):
        for mode in range(2):
            v = place[1 - mode]
            src = xn.at[mode, q, v]
            st["c", q, mode] = [send(src, src, ring(1 - mode, d)) for d in (1, -1)]

    def c_fwd(q):
        for mode in range(2):
            v = place[1 - mode]
            plus, minus = st["c", q, mode]
            plus.wait_recv()
            src = xn.at[mode, q, up(v, -1), pl.ds(0, 128)]
            ahead_copy = send(src, src, ring(1 - mode, 1))
            minus.wait_recv()
            src = xn.at[mode, q, up(v, 1), pl.ds(128, 128)]
            st["cf", q, mode] = (ahead_copy, send(src, src, ring(1 - mode, -1)))

    def c_fin(q):
        for mode in range(2):
            for copy in st["cf", q, mode]:
                copy.wait_recv()

    def d_send(k):
        src = yg.at[place_of(k), pl.ds(k * rows, rows)]
        st["dp", k] = send(src, src, ring(k % 2, 1))
        st["dm", k] = send(src, src, ring(k % 2, -1))

    def d_fwd(k):
        st["dp", k].wait_recv()
        src = yg.at[up(place_of(k), -1), pl.ds(k * rows, half)]
        st["dfp", k] = send(src, src, ring(k % 2, 1))
        st["dm", k].wait_recv()
        src = yg.at[up(place_of(k), 1), pl.ds(k * rows + half, half)]
        st["dfm", k] = send(src, src, ring(k % 2, -1))

    def pair(k):
        st["dfp", k].wait_recv()
        st["dfm", k].wait_recv()
        mode = k % 2
        for h in (o, c):
            total = None
            for q in range(3):
                lhs = yg[:, k * rows:(k + 1) * rows, q * TILE:(q + 1) * TILE]
                rhs = xn[mode, q, pl.ds(2 * h, 2)]
                term = nt(lhs.reshape(4 * rows, TILE), rhs.reshape(2 * BLK, TILE))
                total = term if total is None else total + term
            pch[k, h] = total
            if h is o:
                st["e1", k] = send(pch.at[k, o], crecv.at[k], core_peer)

    def e2(k):
        st["e1", k].wait_recv()
        total = pch[k, c] + crecv[k]
        pch[k, c] = total
        ysend[k] = total.astype(BF16).reshape(4, rows, TILE)
        for d in (2, 1, 3):
            st["e2", k, d] = send(
                ysend.at[k, up(y, d)], yrecv.at[k, d - 1], y_of(y + d)
            )

    def e3(k):
        part = pl.ds(pl.multiple_of(y * rows, rows), rows)
        total = pch[k, c, part, :]
        for d in (1, 2, 3):
            st["e2", k, d].wait_recv()
            total = total + yrecv[k, d - 1].astype(F32)
        eye0 = lax.broadcasted_iota(jnp.int32, (rows, BLK), 0) + k * rows
        eye1 = lax.broadcasted_iota(jnp.int32, (rows, BLK), 1)
        eye = eye0 == eye1
        mu_block = y * 4 + x if k % 2 == 0 else z * 4 + y
        sides = []
        mu_at = [
            jnp.sum(jnp.where(eye, pos[a, pl.ds(mu_block, 1), :], 0.0), axis=1, keepdims=True)
            for a in range(3)
        ]
        for h in range(2):
            nu_block = z * 4 + 2 * c + h if k % 2 == 0 else (2 * c + h) * 4 + x
            dist = jnp.ones((rows, BLK), F32)
            for a in range(3):
                delta = mu_at[a] - pos[a, pl.ds(nu_block, 1), :]
                dist = dist + delta * delta
            sides.append(lax.rsqrt(dist))
        kern = jnp.concatenate(sides, axis=1)
        sfull[k, c, y] = (total * kern).astype(BF16)
        src = sfull.at[k, c, y]
        for d in (2, 1, 3):
            st["e3", k, d] = send(src, src, y_of(y + d))

    def e4(k):
        for d in (1, 2, 3):
            st["e3", k, d].wait_recv()
        src = sfull.at[k, c]
        st["e4", k] = send(src, src, core_peer)

    def res(k):
        st["e4", k].wait_recv()
        mode = k % 2
        lhs = [sfull[k, h].reshape(4 * rows, 2 * BLK) for h in range(2)]
        for q in range(3):
            total = nn(lhs[0], xn[mode, q, 0:2].reshape(2 * BLK, TILE))
            total = total + nn(lhs[1], xn[mode, q, 2:4].reshape(2 * BLK, TILE))
            cut = slice(q * TILE, (q + 1) * TILE)
            rpart[k, :, :, cut] = total.reshape(4, rows, TILE)
            fsend[k, :, :, cut] = total.astype(BF16).reshape(4, rows, TILE)
        v = place_of(k)
        far_v, up_v, dn_v = up(v, 2), up(v, 1), up(v, -1)
        lo, hi = pl.ds(0, half), pl.ds(half, half)
        st["fp", k] = send(fsend.at[k, far_v, lo], ffwd.at[k, 0], ring(mode, 1))
        st["fm", k] = send(fsend.at[k, far_v, hi], ffwd.at[k, 1], ring(mode, -1))
        st["fdp", k] = send(fsend.at[k, up_v, hi], frecv.at[k, 0], ring(mode, 1))
        st["fdm", k] = send(fsend.at[k, dn_v, lo], frecv.at[k, 1], ring(mode, -1))

    def f_fwd(k):
        up_v, dn_v = up(place_of(k), 1), up(place_of(k), -1)
        st["fp", k].wait_recv()
        fsum[k, 0] = (rpart[k, up_v, 0:half, :] + ffwd[k, 0].astype(F32)).astype(BF16)
        st["fsp", k] = send(fsum.at[k, 0], frecv.at[k, 2], ring(k % 2, 1))
        st["fm", k].wait_recv()
        fsum[k, 1] = (rpart[k, dn_v, half:rows, :] + ffwd[k, 1].astype(F32)).astype(BF16)
        st["fsm", k] = send(fsum.at[k, 1], frecv.at[k, 3], ring(k % 2, -1))

    def f_fin(k):
        v = place_of(k)
        for name in ("fdp", "fdm", "fsp", "fsm"):
            st[name, k].wait_recv()
        lo = rpart[k, v, 0:half, :] + frecv[k, 2].astype(F32) + frecv[k, 1].astype(F32)
        hi = rpart[k, v, half:rows, :] + frecv[k, 0].astype(F32) + frecv[k, 3].astype(F32)
        out_ref[k * rows:k * rows + half, :] = lo.astype(BF16)
        out_ref[k * rows + half:(k + 1) * rows, :] = hi.astype(BF16)

    steps = [(a_send, s) for s in range(WINDOW, min(12, WINDOW + 4))]
    steps += [(a_fin, 0)] + [(b_send, 0, k) for k in range(NCH)] + [(c_send, 0)]
    steps += [(a_send, s) for s in range(WINDOW + 4, 12)]
    steps += [(a_fin, 1)] + [(b_send, 1, k) for k in range(NCH)] + [(c_send, 1)]
    steps += [(a_fin, 2), (b_send, 2, 0), (b_send, 2, 1), (c_send, 2), (c_fwd, 0)]
    steps += [(b_core, 0, k) for k in range(NCH)] + [(c_fwd, 1)]
    steps += [(b_core, 1, k) for k in range(NCH)]
    steps += [
        (b_core, 2, 0), (b_send, 2, 2), (y_stage, 0), (d_send, 0),
        (b_core, 2, 1), (b_send, 2, 3), (c_fwd, 2), (y_stage, 1), (d_send, 1),
        (b_core, 2, 2), (d_fwd, 0), (y_stage, 2), (d_send, 2),
        (b_core, 2, 3), (d_fwd, 1), (y_stage, 3), (d_send, 3),
        (c_fin, 0), (c_fin, 1), (c_fin, 2),
        (pair, 0), (pair, 1), (d_fwd, 2), (e2, 0), (e2, 1), (d_fwd, 3),
        (e3, 0), (pair, 2), (e3, 1), (pair, 3),
        (e4, 0), (e2, 2), (e4, 1), (e2, 3),
        (res, 0), (e3, 2), (res, 1), (e3, 3), (e4, 2), (e4, 3),
        (f_fwd, 0), (f_fwd, 1), (res, 2), (res, 3), (f_fwd, 2), (f_fwd, 3),
    ]
    steps += [(f_fin, k) for k in range(NCH)]
    for stage, *at in steps:
        stage(*at)
    for copy in open_sends:
        copy.wait_send()


def local(orbitals, point_owner, point_row, density_tiles, tile_columns, tile_counts):
    rows = BLK // NCH
    half = rows // 2
    vmem = pl.BlockSpec(memory_space=pltpu.VMEM)
    smem = pl.BlockSpec(memory_space=pltpu.SMEM)
    hbm = pl.BlockSpec(memory_space=pl.ANY)
    return pl.pallas_call(
        kernel,
        name="exchange",
        out_shape=jax.ShapeDtypeStruct((BLK, COLS), BF16),
        in_specs=[vmem, smem, smem, hbm, hbm],
        out_specs=vmem,
        scratch_shapes=[
            pltpu.VMEM((1024, COLS), BF16),
            pltpu.VMEM((18, TILE, TILE), BF16),
            pltpu.VMEM((512, 1024), BF16),
            pltpu.VMEM((3, 512, TILE), BF16),
            pltpu.VMEM((3, 512, TILE), BF16),
            pltpu.VMEM((2, 3, 4, BLK, TILE), BF16),
            pltpu.VMEM((24, rows, TILE), BF16),
            pltpu.VMEM((24, rows, TILE), BF16),
            pltpu.VMEM((24, rows, TILE), BF16),
            pltpu.VMEM((24, rows, TILE), BF16),
            pltpu.VMEM((4, BLK, COLS), BF16),
            pltpu.VMEM((NCH, 2, 4 * rows, TILE), F32),
            pltpu.VMEM((NCH, 4 * rows, TILE), F32),
            pltpu.VMEM((NCH, 4, rows, TILE), BF16),
            pltpu.VMEM((NCH, 3, rows, TILE), BF16),
            pltpu.VMEM((NCH, 2, 4, rows, TILE), BF16),
            pltpu.VMEM((NCH, 4, rows, COLS), F32),
            pltpu.VMEM((NCH, 4, rows, COLS), BF16),
            pltpu.VMEM((NCH, 4, half, COLS), BF16),
            pltpu.VMEM((NCH, 2, half, COLS), BF16),
            pltpu.VMEM((NCH, 2, half, COLS), BF16),
            pltpu.VMEM((3, 16, BLK), F32),
            pltpu.SemaphoreType.DMA((NSEM,)),
            pltpu.SemaphoreType.DMA((NSEM,)),
            pltpu.SemaphoreType.DMA((2,)),
        ],
        compiler_params=pltpu.CompilerParams(
            collective_id=0, has_side_effects=True, vmem_limit_bytes=60 * 2**20
        ),
        cost_estimate=pl.CostEstimate(
            flops=12_000_000_000, bytes_accessed=14_000_000, transcendentals=0
        ),
    )(
        (point_owner[:, 0] * 1024 + point_row).reshape(16, BLK),
        tile_columns,
        tile_counts,
        orbitals,
        density_tiles.reshape(18, TILE, TILE),
    )


def solution(mesh):
    in_specs = (
        P("grid", "band"),
        P(),
        P(),
        P("band", None, None, None),
        P("band", None),
        P("band"),
    )
    return jax.shard_map(
        local, mesh=mesh, in_specs=in_specs, out_specs=P("grid", "band"), check_vma=False
    )
```

```python
import functools

import jax
import jax.numpy as jnp
from jax import lax
from jax.experimental import pallas as pl
from jax.experimental.pallas import tpu as pltpu
from jax.sharding import PartitionSpec as P

MESH = pl.DeviceIdType.MESH
F32 = jnp.float32
BF16 = jnp.bfloat16
NCH = 4
BLK = 256
COLS = 1536
TILE = 512
CAP = 32
NSEM = 200
FORWARDED = 3
WINDOW = 5


def nt(a, b):
    return lax.dot_general(a, b, (((1,), (1,)), ((), ())), preferred_element_type=F32)


def nn(a, b):
    return lax.dot_general(a, b, (((1,), (0,)), ((), ())), preferred_element_type=F32)


def kernel(
    index_ref, cols_ref, counts_ref, orb_hbm, tiles_hbm, out_ref,
    orb, tiles, onehot, slots_out, slots_in, xn, ev0, ev1, yg,
    pch, crecv, ysend, yrecv, sfull, rpart, fsend, frecv, ffwd, fsum, pos,
    ss, rs, ls,
):
    every = (ev0, ev1)
    rows = BLK // NCH
    half = rows // 2
    g = lax.axis_index("grid")
    b = lax.axis_index("band")
    z, x, y, c = g // 4, g % 4, b // 2, b % 2
    o = 1 - c

    def grid_of(zz, xx):
        return (((zz + 4) % 4) * 4 + (xx + 4) % 4, b)

    def y_of(yy):
        return (g, ((yy + 4) % 4) * 2 + c)

    core_peer = (g, y * 2 + o)
    up = lambda v, d: (v + d + 4) % 4

    place = (z, x)

    def ring(mode, d):
        return grid_of(z + d, x) if mode == 0 else grid_of(z, x + d)

    counter = [0]
    open_sends = []

    def send(src, dst, to):
        k = counter[0]
        counter[0] += 1
        copy = pltpu.make_async_remote_copy(
            src_ref=src, dst_ref=dst, send_sem=ss.at[k], recv_sem=rs.at[k],
            device_id=to, device_id_type=MESH,
        )
        copy.start()
        open_sends.append(copy)
        return copy

    bar = pltpu.get_barrier_semaphore()
    for dz in (2, 1, 3, 0):
        for dx in (2, 1, 3, 0):
            if (dz, dx) != (0, 0):
                pl.semaphore_signal(
                    bar, inc=1, device_id=grid_of(z + dz, x + dx), device_id_type=MESH
                )
    for dy in (1, 2, 3):
        pl.semaphore_signal(bar, inc=1, device_id=y_of(y + dy), device_id_type=MESH)
    pl.semaphore_signal(bar, inc=1, device_id=core_peer, device_id_type=MESH)

    load_orb = pltpu.make_async_copy(orb_hbm, orb, ls.at[0])
    load_orb.start()
    load_tiles = pltpu.make_async_copy(tiles_hbm, tiles, ls.at[1])
    load_tiles.start()

    index = index_ref[...]
    owner = index // 1024
    rowf = (index % 1024).astype(F32)
    holder = (owner == g).astype(F32)
    p0 = lax.broadcasted_iota(jnp.int32, (BLK, BLK), 0)
    p1 = lax.broadcasted_iota(jnp.int32, (BLK, BLK), 1)
    before = (p0 < p1).astype(BF16)
    ahead = nn(holder.astype(BF16), before)
    slot_id = lax.broadcasted_iota(jnp.int32, (CAP, BLK), 0).astype(F32)
    grid_row = lax.broadcasted_iota(jnp.int32, (CAP, 1024), 1).astype(F32)
    for i in range(16):
        picked = (ahead[i:i + 1, :] == slot_id) & (holder[i:i + 1, :] > 0.5)
        wanted = jnp.sum(jnp.where(picked, rowf[i:i + 1, :], 0.0), axis=1, keepdims=True)
        onehot[i * CAP:(i + 1) * CAP, :] = (grid_row == wanted).astype(F32).astype(BF16)

    load_orb.wait()
    mine = pl.ds(pl.multiple_of(g * CAP, CAP), CAP)
    groups = (
        ((2, 1), (2, 3), (1, 2), (3, 2)),
        ((2, 0), (0, 2), (2, 2)),
        ((1, 1), (3, 3), (1, 3), (3, 1)),
        ((1, 0), (3, 0), (0, 1), (0, 3)),
    )
    pieces = [(q, group) for q in range(3) for group in groups]
    a_copies = []

    def a_rows(q):
        slots_out[q] = nn(onehot[...], orb[:, q * TILE:(q + 1) * TILE]).astype(BF16)
        slots_in[q, mine, :] = slots_out[q, mine, :]

    def a_send(s):
        if s >= WINDOW:
            for copy in a_copies[s - WINDOW]:
                copy.wait_send()
                open_sends[:] = [other for other in open_sends if other is not copy]
        q, group = pieces[s]
        sent = []
        for dz, dx in group:
            to = grid_of(z + dz, x + dx)
            src = pl.ds(pl.multiple_of(to[0] * CAP, CAP), CAP)
            sent.append(send(slots_out.at[q, src], slots_in.at[q, mine], to))
        a_copies.append(sent)

    a_rows(0)
    pl.semaphore_wait(bar, 19)
    for s in range(min(WINDOW, 4)):
        a_send(s)
    a_rows(1)
    for s in range(4, WINDOW):
        a_send(s)
    a_rows(2)

    pos[0] = (index % 16).astype(F32)
    pos[1] = (index // 16 % 16).astype(F32)
    pos[2] = (index // 256).astype(F32)
    own_row = (index_ref[pl.ds(g, 1), :] // 1024).astype(F32)
    own_col = jnp.sum(jnp.where(p0 == p1, own_row, 0.0), axis=1, keepdims=True)
    rank = jnp.sum(
        jnp.where((own_row == own_col) & (p1 < p0), 1.0, 0.0), axis=1, keepdims=True
    )
    flat = own_col * CAP + rank
    slot_no = lax.broadcasted_iota(jnp.int32, (BLK, 16 * CAP), 1).astype(F32)
    unpermute = (slot_no == flat).astype(F32).astype(BF16)

    st = {}

    def a_fin(q):
        for group in a_copies[4 * q:4 * q + 4]:
            for copy in group:
                copy.wait_recv()
        points = nn(unpermute, slots_in[q]).astype(BF16)
        xn[0, q, x] = points
        xn[1, q, z] = points
        for m in range(2):
            every[m][c * 12 + q * 4 + y] = points[m * 128:(m + 1) * 128, :]

    def b_send(q, m):
        src = every[m].at[c * 12 + q * 4 + y]
        ways = (1, 3) if q < FORWARDED else (2, 1, 3)
        st["b", q, m] = [send(src, src, y_of(y + d)) for d in ways]

    def b_fwd(q, m):
        plus, minus = st["b", q, m]
        plus.wait_recv()
        src = every[m].at[c * 12 + q * 4 + up(y, -1), pl.ds(0, 64)]
        forwarded = [send(src, src, y_of(y + 1))]
        minus.wait_recv()
        src = every[m].at[c * 12 + q * 4 + up(y, 1), pl.ds(64, 64)]
        st["b", q, m] = forwarded + [send(src, src, y_of(y - 1))]

    def b_core(q, m):
        for copy in st["b", q, m]:
            copy.wait_recv()
        src = every[m].at[pl.ds(c * 12 + q * 4, 4)]
        st["bc", q, m] = send(src, src, core_peer)

    def y_stage(m):
        for q in range(3):
            st["bc", q, m].wait_recv()
        if m == 0:
            load_tiles.wait()
        for r in range(3):
            acc = jnp.zeros((128, TILE), F32)
            count = counts_ref[r]
            for s in range(6):
                col = cols_ref[r, s]
                block = every[m][(col // 3 % 2) * 12 + (col % 3) * 4 + col // 6]
                if s > 0:
                    keep = (count > s).astype(F32)
                    block = block * keep.astype(BF16)
                acc = acc + nt(block, tiles[r * 6 + s])
            acc = acc.astype(BF16)
            cut = slice(r * TILE, (r + 1) * TILE)
            yg[z, m * 128:m * 128 + 64, cut] = acc[:64]
            yg[x, m * 128 + 64:m * 128 + 128, cut] = acc[64:]

    def place_of(k):
        return place[k % 2]

    def c_send(q):
        for mode in range(2):
            v = place[1 - mode]
            src = xn.at[mode, q, v]
            st["c", q, mode] = [send(src, src, ring(1 - mode, d)) for d in (1, -1)]

    def c_fwd(q):
        for mode in range(2):
            v = place[1 - mode]
            plus, minus = st["c", q, mode]
            plus.wait_recv()
            src = xn.at[mode, q, up(v, -1), pl.ds(0, 128)]
            ahead_copy = send(src, src, ring(1 - mode, 1))
            minus.wait_recv()
            src = xn.at[mode, q, up(v, 1), pl.ds(128, 128)]
            st["cf", q, mode] = (ahead_copy, send(src, src, ring(1 - mode, -1)))

    def c_fin(q):
        for mode in range(2):
            for copy in st["cf", q, mode]:
                copy.wait_recv()

    def d_send(k):
        src = yg.at[place_of(k), pl.ds(k * rows, rows)]
        st["dp", k] = send(src, src, ring(k % 2, 1))
        st["dm", k] = send(src, src, ring(k % 2, -1))

    def d_fwd(k):
        st["dp", k].wait_recv()
        src = yg.at[up(place_of(k), -1), pl.ds(k * rows, half)]
        st["dfp", k] = send(src, src, ring(k % 2, 1))
        st["dm", k].wait_recv()
        src = yg.at[up(place_of(k), 1), pl.ds(k * rows + half, half)]
        st["dfm", k] = send(src, src, ring(k % 2, -1))

    def pair(k):
        st["dfp", k].wait_recv()
        st["dfm", k].wait_recv()
        mode = k % 2
        for h in (o, c):
            total = None
            for q in range(3):
                lhs = yg[:, k * rows:(k + 1) * rows, q * TILE:(q + 1) * TILE]
                rhs = xn[mode, q, pl.ds(2 * h, 2)]
                term = nt(lhs.reshape(4 * rows, TILE), rhs.reshape(2 * BLK, TILE))
                total = term if total is None else total + term
            pch[k, h] = total
            if h is o:
                st["e1", k] = send(pch.at[k, o], crecv.at[k], core_peer)

    def e2(k):
        st["e1", k].wait_recv()
        total = pch[k, c] + crecv[k]
        pch[k, c] = total
        ysend[k] = total.astype(BF16).reshape(4, rows, TILE)
        for d in (2, 1, 3):
            st["e2", k, d] = send(
                ysend.at[k, up(y, d)], yrecv.at[k, d - 1], y_of(y + d)
            )

    def e3(k):
        part = pl.ds(pl.multiple_of(y * rows, rows), rows)
        total = pch[k, c, part, :]
        for d in (1, 2, 3):
            st["e2", k, d].wait_recv()
            total = total + yrecv[k, d - 1].astype(F32)
        eye0 = lax.broadcasted_iota(jnp.int32, (rows, BLK), 0) + k * rows
        eye1 = lax.broadcasted_iota(jnp.int32, (rows, BLK), 1)
        eye = eye0 == eye1
        mu_block = y * 4 + x if k % 2 == 0 else z * 4 + y
        sides = []
        mu_at = [
            jnp.sum(jnp.where(eye, pos[a, pl.ds(mu_block, 1), :], 0.0), axis=1, keepdims=True)
            for a in range(3)
        ]
        for h in range(2):
            nu_block = z * 4 + 2 * c + h if k % 2 == 0 else (2 * c + h) * 4 + x
            dist = jnp.ones((rows, BLK), F32)
            for a in range(3):
                delta = mu_at[a] - pos[a, pl.ds(nu_block, 1), :]
                dist = dist + delta * delta
            sides.append(lax.rsqrt(dist))
        kern = jnp.concatenate(sides, axis=1)
        sfull[k, c, y] = (total * kern).astype(BF16)
        src = sfull.at[k, c, y]
        for d in (2, 1, 3):
            st["e3", k, d] = send(src, src, y_of(y + d))

    def e4(k):
        for d in (1, 2, 3):
            st["e3", k, d].wait_recv()
        src = sfull.at[k, c]
        st["e4", k] = send(src, src, core_peer)

    def res(k):
        st["e4", k].wait_recv()
        mode = k % 2
        lhs = [sfull[k, h].reshape(4 * rows, 2 * BLK) for h in range(2)]
        for q in range(3):
            total = nn(lhs[0], xn[mode, q, 0:2].reshape(2 * BLK, TILE))
            total = total + nn(lhs[1], xn[mode, q, 2:4].reshape(2 * BLK, TILE))
            cut = slice(q * TILE, (q + 1) * TILE)
            rpart[k, :, :, cut] = total.reshape(4, rows, TILE)
            fsend[k, :, :, cut] = total.astype(BF16).reshape(4, rows, TILE)
        v = place_of(k)
        far_v, up_v, dn_v = up(v, 2), up(v, 1), up(v, -1)
        lo, hi = pl.ds(0, half), pl.ds(half, half)
        st["fp", k] = send(fsend.at[k, far_v, lo], ffwd.at[k, 0], ring(mode, 1))
        st["fm", k] = send(fsend.at[k, far_v, hi], ffwd.at[k, 1], ring(mode, -1))
        st["fdp", k] = send(fsend.at[k, up_v, hi], frecv.at[k, 0], ring(mode, 1))
        st["fdm", k] = send(fsend.at[k, dn_v, lo], frecv.at[k, 1], ring(mode, -1))

    def f_fwd(k):
        up_v, dn_v = up(place_of(k), 1), up(place_of(k), -1)
        st["fp", k].wait_recv()
        fsum[k, 0] = (rpart[k, up_v, 0:half, :] + ffwd[k, 0].astype(F32)).astype(BF16)
        st["fsp", k] = send(fsum.at[k, 0], frecv.at[k, 2], ring(k % 2, 1))
        st["fm", k].wait_recv()
        fsum[k, 1] = (rpart[k, dn_v, half:rows, :] + ffwd[k, 1].astype(F32)).astype(BF16)
        st["fsm", k] = send(fsum.at[k, 1], frecv.at[k, 3], ring(k % 2, -1))

    def f_fin(k):
        v = place_of(k)
        for name in ("fdp", "fdm", "fsp", "fsm"):
            st[name, k].wait_recv()
        lo = rpart[k, v, 0:half, :] + frecv[k, 2].astype(F32) + frecv[k, 1].astype(F32)
        hi = rpart[k, v, half:rows, :] + frecv[k, 0].astype(F32) + frecv[k, 3].astype(F32)
        out_ref[k * rows:k * rows + half, :] = lo.astype(BF16)
        out_ref[k * rows + half:(k + 1) * rows, :] = hi.astype(BF16)

    both = range(2)
    steps = [(a_send, s) for s in range(WINDOW, min(12, WINDOW + 4))]
    steps += [(a_fin, 0)] + [(b_send, 0, m) for m in both] + [(c_send, 0)]
    steps += [(a_send, s) for s in range(WINDOW + 4, 12)]
    steps += [(a_fin, 1)] + [(b_send, 1, m) for m in both]
    steps += [(b_fwd, 0, m) for m in both] + [(c_send, 1)]
    steps += [(a_fin, 2), (b_send, 2, 0)] + [(b_fwd, 1, m) for m in both]
    steps += [(b_send, 2, 1), (c_send, 2)]
    steps += [(b_core, q, m) for q in both for m in both]
    steps += [
        (b_fwd, 2, 0), (c_fwd, 0), (b_fwd, 2, 1), (b_core, 2, 0), (c_fwd, 1),
        (y_stage, 0), (d_send, 0), (d_send, 1), (c_fwd, 2),
        (b_core, 2, 1), (y_stage, 1), (d_fwd, 0), (d_fwd, 1), (d_send, 2), (d_send, 3),
        (c_fin, 0), (c_fin, 1), (c_fin, 2),
        (pair, 0), (pair, 1), (e2, 0), (e2, 1), (d_fwd, 2), (d_fwd, 3),
        (e3, 0), (e3, 1), (pair, 2), (pair, 3), (e2, 2), (e4, 0), (e2, 3), (e4, 1),
        (res, 0), (res, 1), (e3, 2), (e3, 3), (f_fwd, 0), (f_fwd, 1),
        (e4, 2), (e4, 3), (res, 2), (res, 3), (f_fin, 0), (f_fin, 1), (f_fwd, 2), (f_fwd, 3),
    ]
    steps += [(f_fin, 2), (f_fin, 3)]
    for stage, *at in steps:
        stage(*at)
    for copy in open_sends:
        copy.wait_send()


def local(orbitals, point_owner, point_row, density_tiles, tile_columns, tile_counts):
    rows = BLK // NCH
    half = rows // 2
    vmem = pl.BlockSpec(memory_space=pltpu.VMEM)
    smem = pl.BlockSpec(memory_space=pltpu.SMEM)
    hbm = pl.BlockSpec(memory_space=pl.ANY)
    return pl.pallas_call(
        kernel,
        name="exchange",
        out_shape=jax.ShapeDtypeStruct((BLK, COLS), BF16),
        in_specs=[vmem, smem, smem, hbm, hbm],
        out_specs=vmem,
        scratch_shapes=[
            pltpu.VMEM((1024, COLS), BF16),
            pltpu.VMEM((18, TILE, TILE), BF16),
            pltpu.VMEM((512, 1024), BF16),
            pltpu.VMEM((3, 512, TILE), BF16),
            pltpu.VMEM((3, 512, TILE), BF16),
            pltpu.VMEM((2, 3, 4, BLK, TILE), BF16),
            pltpu.VMEM((24, 128, TILE), BF16),
            pltpu.VMEM((24, 128, TILE), BF16),
            pltpu.VMEM((4, BLK, COLS), BF16),
            pltpu.VMEM((NCH, 2, 4 * rows, TILE), F32),
            pltpu.VMEM((NCH, 4 * rows, TILE), F32),
            pltpu.VMEM((NCH, 4, rows, TILE), BF16),
            pltpu.VMEM((NCH, 3, rows, TILE), BF16),
            pltpu.VMEM((NCH, 2, 4, rows, TILE), BF16),
            pltpu.VMEM((NCH, 4, rows, COLS), F32),
            pltpu.VMEM((NCH, 4, rows, COLS), BF16),
            pltpu.VMEM((NCH, 4, half, COLS), BF16),
            pltpu.VMEM((NCH, 2, half, COLS), BF16),
            pltpu.VMEM((NCH, 2, half, COLS), BF16),
            pltpu.VMEM((3, 16, BLK), F32),
            pltpu.SemaphoreType.DMA((NSEM,)),
            pltpu.SemaphoreType.DMA((NSEM,)),
            pltpu.SemaphoreType.DMA((2,)),
        ],
        compiler_params=pltpu.CompilerParams(
            collective_id=0, has_side_effects=True, vmem_limit_bytes=60 * 2**20
        ),
        cost_estimate=pl.CostEstimate(
            flops=12_000_000_000, bytes_accessed=14_000_000, transcendentals=0
        ),
    )(
        (point_owner[:, 0] * 1024 + point_row).reshape(16, BLK),
        tile_columns,
        tile_counts,
        orbitals,
        density_tiles.reshape(18, TILE, TILE),
    )


def solution(mesh):
    in_specs = (
        P("grid", "band"),
        P(),
        P(),
        P("band", None, None, None),
        P("band", None),
        P("band"),
    )
    return jax.shard_map(
        local, mesh=mesh, in_specs=in_specs, out_specs=P("grid", "band"), check_vma=False
    )
```

```python
import functools

import jax
import jax.numpy as jnp
from jax import lax
from jax.experimental import pallas as pl
from jax.experimental.pallas import tpu as pltpu
from jax.sharding import PartitionSpec as P

MESH = pl.DeviceIdType.MESH
F32 = jnp.float32
BF16 = jnp.bfloat16
NCH = 4
BLK = 256
COLS = 1536
TILE = 512
CAP = 32
NSEM = 200
FORWARDED = 3
WINDOW = 5


def nt(a, b):
    return lax.dot_general(a, b, (((1,), (1,)), ((), ())), preferred_element_type=F32)


def nn(a, b):
    return lax.dot_general(a, b, (((1,), (0,)), ((), ())), preferred_element_type=F32)


def kernel(
    index_ref, cols_ref, counts_ref, orb_hbm, tiles_hbm, out_ref,
    orb, tiles, onehot, slots_out, slots_in, xn, ev0, ev1, yg,
    pch, crecv, ysend, yrecv, sfull, rpart, fsend, frecv, ffwd, fsum, pos,
    ss, rs, ls,
):
    every = (ev0, ev1)
    rows = BLK // NCH
    half = rows // 2
    g = lax.axis_index("grid")
    b = lax.axis_index("band")
    z, x, y, c = g // 4, g % 4, b // 2, b % 2
    o = 1 - c

    def grid_of(zz, xx):
        return (((zz + 4) % 4) * 4 + (xx + 4) % 4, b)

    def y_of(yy):
        return (g, ((yy + 4) % 4) * 2 + c)

    core_peer = (g, y * 2 + o)
    up = lambda v, d: (v + d + 4) % 4

    place = (z, x)

    def ring(mode, d):
        return grid_of(z + d, x) if mode == 0 else grid_of(z, x + d)

    counter = [0]
    open_sends = []

    def send(src, dst, to):
        k = counter[0]
        counter[0] += 1
        copy = pltpu.make_async_remote_copy(
            src_ref=src, dst_ref=dst, send_sem=ss.at[k], recv_sem=rs.at[k],
            device_id=to, device_id_type=MESH,
        )
        copy.start()
        open_sends.append(copy)
        return copy

    load_orb = pltpu.make_async_copy(orb_hbm, orb, ls.at[0])
    load_orb.start()

    bar = pltpu.get_barrier_semaphore()
    for dz in (2, 1, 3, 0):
        for dx in (2, 1, 3, 0):
            if (dz, dx) != (0, 0):
                pl.semaphore_signal(
                    bar, inc=1, device_id=grid_of(z + dz, x + dx), device_id_type=MESH
                )
    for dy in (1, 2, 3):
        pl.semaphore_signal(bar, inc=1, device_id=y_of(y + dy), device_id_type=MESH)
    pl.semaphore_signal(bar, inc=1, device_id=core_peer, device_id_type=MESH)


    index = index_ref[...]
    owner = index // 1024
    rowf = (index % 1024).astype(F32)
    holder = (owner == g).astype(F32)
    p0 = lax.broadcasted_iota(jnp.int32, (BLK, BLK), 0)
    p1 = lax.broadcasted_iota(jnp.int32, (BLK, BLK), 1)
    before = (p0 < p1).astype(BF16)
    ahead = nn(holder.astype(BF16), before)
    slot_id = lax.broadcasted_iota(jnp.int32, (CAP, BLK), 0).astype(F32)
    grid_row = lax.broadcasted_iota(jnp.int32, (CAP, 1024), 1).astype(F32)
    for i in range(16):
        picked = (ahead[i:i + 1, :] == slot_id) & (holder[i:i + 1, :] > 0.5)
        wanted = jnp.sum(jnp.where(picked, rowf[i:i + 1, :], 0.0), axis=1, keepdims=True)
        onehot[i * CAP:(i + 1) * CAP, :] = (grid_row == wanted).astype(F32).astype(BF16)

    load_orb.wait()
    load_tiles = pltpu.make_async_copy(tiles_hbm, tiles, ls.at[1])
    load_tiles.start()
    mine = pl.ds(pl.multiple_of(g * CAP, CAP), CAP)
    groups = (
        ((2, 1), (2, 3), (1, 2), (3, 2)),
        ((2, 0), (0, 2), (2, 2)),
        ((1, 1), (3, 3), (1, 3), (3, 1)),
        ((1, 0), (3, 0), (0, 1), (0, 3)),
    )
    pieces = [(q, group) for q in range(3) for group in groups]
    a_copies = []

    def a_rows(q):
        slots_out[q] = nn(onehot[...], orb[:, q * TILE:(q + 1) * TILE]).astype(BF16)
        slots_in[q, mine, :] = slots_out[q, mine, :]

    def a_send(s):
        if s >= WINDOW:
            for copy in a_copies[s - WINDOW]:
                copy.wait_send()
                open_sends[:] = [other for other in open_sends if other is not copy]
        q, group = pieces[s]
        sent = []
        for dz, dx in group:
            to = grid_of(z + dz, x + dx)
            src = pl.ds(pl.multiple_of(to[0] * CAP, CAP), CAP)
            sent.append(send(slots_out.at[q, src], slots_in.at[q, mine], to))
        a_copies.append(sent)

    a_rows(0)
    pl.semaphore_wait(bar, 19)
    for s in range(min(WINDOW, 4)):
        a_send(s)
    a_rows(1)
    for s in range(4, WINDOW):
        a_send(s)
    a_rows(2)

    pos[0] = (index % 16).astype(F32)
    pos[1] = (index // 16 % 16).astype(F32)
    pos[2] = (index // 256).astype(F32)
    own_row = (index_ref[pl.ds(g, 1), :] // 1024).astype(F32)
    own_col = jnp.sum(jnp.where(p0 == p1, own_row, 0.0), axis=1, keepdims=True)
    rank = jnp.sum(
        jnp.where((own_row == own_col) & (p1 < p0), 1.0, 0.0), axis=1, keepdims=True
    )
    flat = own_col * CAP + rank
    slot_no = lax.broadcasted_iota(jnp.int32, (BLK, 16 * CAP), 1).astype(F32)
    unpermute = (slot_no == flat).astype(F32).astype(BF16)

    st = {}

    def a_fin(q):
        for group in a_copies[4 * q:4 * q + 4]:
            for copy in group:
                copy.wait_recv()
        points = nn(unpermute, slots_in[q]).astype(BF16)
        xn[0, q, x] = points
        xn[1, q, z] = points
        for m in range(2):
            every[m][c * 12 + q * 4 + y] = points[m * 128:(m + 1) * 128, :]

    def b_send(q, m):
        src = every[m].at[c * 12 + q * 4 + y]
        ways = (1, 3) if q < FORWARDED else (2, 1, 3)
        st["b", q, m] = [send(src, src, y_of(y + d)) for d in ways]

    def b_fwd(q, m):
        plus, minus = st["b", q, m]
        plus.wait_recv()
        src = every[m].at[c * 12 + q * 4 + up(y, -1), pl.ds(0, 64)]
        forwarded = [send(src, src, y_of(y + 1))]
        minus.wait_recv()
        src = every[m].at[c * 12 + q * 4 + up(y, 1), pl.ds(64, 64)]
        st["b", q, m] = forwarded + [send(src, src, y_of(y - 1))]

    def b_core(q, m):
        for copy in st["b", q, m]:
            copy.wait_recv()
        src = every[m].at[pl.ds(c * 12 + q * 4, 4)]
        st["bc", q, m] = send(src, src, core_peer)

    def y_stage(m):
        for q in range(3):
            st["bc", q, m].wait_recv()
        if m == 0:
            load_tiles.wait()
        for r in range(3):
            acc = jnp.zeros((128, TILE), F32)
            count = counts_ref[r]
            for s in range(6):
                col = cols_ref[r, s]
                block = every[m][(col // 3 % 2) * 12 + (col % 3) * 4 + col // 6]
                if s > 0:
                    keep = (count > s).astype(F32)
                    block = block * keep.astype(BF16)
                acc = acc + nt(block, tiles[r * 6 + s])
            acc = acc.astype(BF16)
            cut = slice(r * TILE, (r + 1) * TILE)
            yg[z, m * 128:m * 128 + 64, cut] = acc[:64]
            yg[x, m * 128 + 64:m * 128 + 128, cut] = acc[64:]

    def place_of(k):
        return place[k % 2]

    def c_send(q):
        for mode in range(2):
            v = place[1 - mode]
            src = xn.at[mode, q, v]
            st["c", q, mode] = [send(src, src, ring(1 - mode, d)) for d in (1, -1)]

    def c_fwd(q):
        for mode in range(2):
            v = place[1 - mode]
            plus, minus = st["c", q, mode]
            plus.wait_recv()
            src = xn.at[mode, q, up(v, -1), pl.ds(0, 128)]
            ahead_copy = send(src, src, ring(1 - mode, 1))
            minus.wait_recv()
            src = xn.at[mode, q, up(v, 1), pl.ds(128, 128)]
            st["cf", q, mode] = (ahead_copy, send(src, src, ring(1 - mode, -1)))

    def c_fin(q):
        for mode in range(2):
            for copy in st["cf", q, mode]:
                copy.wait_recv()

    def d_send(k):
        src = yg.at[place_of(k), pl.ds(k * rows, rows)]
        st["dp", k] = send(src, src, ring(k % 2, 1))
        st["dm", k] = send(src, src, ring(k % 2, -1))

    def d_fwd(k):
        st["dp", k].wait_recv()
        src = yg.at[up(place_of(k), -1), pl.ds(k * rows, half)]
        st["dfp", k] = send(src, src, ring(k % 2, 1))
        st["dm", k].wait_recv()
        src = yg.at[up(place_of(k), 1), pl.ds(k * rows + half, half)]
        st["dfm", k] = send(src, src, ring(k % 2, -1))

    def pair(k):
        st["dfp", k].wait_recv()
        st["dfm", k].wait_recv()
        mode = k % 2
        for h in (o, c):
            total = None
            for q in range(3):
                lhs = yg[:, k * rows:(k + 1) * rows, q * TILE:(q + 1) * TILE]
                rhs = xn[mode, q, pl.ds(2 * h, 2)]
                term = nt(lhs.reshape(4 * rows, TILE), rhs.reshape(2 * BLK, TILE))
                total = term if total is None else total + term
            pch[k, h] = total
            if h is o:
                st["e1", k] = send(pch.at[k, o], crecv.at[k], core_peer)

    def e2(k):
        st["e1", k].wait_recv()
        total = pch[k, c] + crecv[k]
        pch[k, c] = total
        ysend[k] = total.astype(BF16).reshape(4, rows, TILE)
        for d in (2, 1, 3):
            st["e2", k, d] = send(
                ysend.at[k, up(y, d)], yrecv.at[k, d - 1], y_of(y + d)
            )

    def e3(k):
        part = pl.ds(pl.multiple_of(y * rows, rows), rows)
        total = pch[k, c, part, :]
        for d in (1, 2, 3):
            st["e2", k, d].wait_recv()
            total = total + yrecv[k, d - 1].astype(F32)
        eye0 = lax.broadcasted_iota(jnp.int32, (rows, BLK), 0) + k * rows
        eye1 = lax.broadcasted_iota(jnp.int32, (rows, BLK), 1)
        eye = eye0 == eye1
        mu_block = y * 4 + x if k % 2 == 0 else z * 4 + y
        sides = []
        mu_at = [
            jnp.sum(jnp.where(eye, pos[a, pl.ds(mu_block, 1), :], 0.0), axis=1, keepdims=True)
            for a in range(3)
        ]
        for h in range(2):
            nu_block = z * 4 + 2 * c + h if k % 2 == 0 else (2 * c + h) * 4 + x
            dist = jnp.ones((rows, BLK), F32)
            for a in range(3):
                delta = mu_at[a] - pos[a, pl.ds(nu_block, 1), :]
                dist = dist + delta * delta
            sides.append(lax.rsqrt(dist))
        kern = jnp.concatenate(sides, axis=1)
        sfull[k, c, y] = (total * kern).astype(BF16)
        src = sfull.at[k, c, y]
        for d in (2, 1, 3):
            st["e3", k, d] = send(src, src, y_of(y + d))

    def e4(k):
        for d in (1, 2, 3):
            st["e3", k, d].wait_recv()
        src = sfull.at[k, c]
        st["e4", k] = send(src, src, core_peer)

    def res(k):
        st["e4", k].wait_recv()
        mode = k % 2
        lhs = [sfull[k, h].reshape(4 * rows, 2 * BLK) for h in range(2)]
        for q in range(3):
            total = nn(lhs[0], xn[mode, q, 0:2].reshape(2 * BLK, TILE))
            total = total + nn(lhs[1], xn[mode, q, 2:4].reshape(2 * BLK, TILE))
            cut = slice(q * TILE, (q + 1) * TILE)
            rpart[k, :, :, cut] = total.reshape(4, rows, TILE)
            fsend[k, :, :, cut] = total.astype(BF16).reshape(4, rows, TILE)
        v = place_of(k)
        far_v, up_v, dn_v = up(v, 2), up(v, 1), up(v, -1)
        lo, hi = pl.ds(0, half), pl.ds(half, half)
        st["fp", k] = send(fsend.at[k, far_v, lo], ffwd.at[k, 0], ring(mode, 1))
        st["fm", k] = send(fsend.at[k, far_v, hi], ffwd.at[k, 1], ring(mode, -1))
        st["fdp", k] = send(fsend.at[k, up_v, hi], frecv.at[k, 0], ring(mode, 1))
        st["fdm", k] = send(fsend.at[k, dn_v, lo], frecv.at[k, 1], ring(mode, -1))

    def f_fwd(k):
        up_v, dn_v = up(place_of(k), 1), up(place_of(k), -1)
        st["fp", k].wait_recv()
        fsum[k, 0] = (rpart[k, up_v, 0:half, :] + ffwd[k, 0].astype(F32)).astype(BF16)
        st["fsp", k] = send(fsum.at[k, 0], frecv.at[k, 2], ring(k % 2, 1))
        st["fm", k].wait_recv()
        fsum[k, 1] = (rpart[k, dn_v, half:rows, :] + ffwd[k, 1].astype(F32)).astype(BF16)
        st["fsm", k] = send(fsum.at[k, 1], frecv.at[k, 3], ring(k % 2, -1))

    def f_fin(k):
        v = place_of(k)
        for name in ("fdp", "fdm", "fsp", "fsm"):
            st[name, k].wait_recv()
        lo = rpart[k, v, 0:half, :] + frecv[k, 2].astype(F32) + frecv[k, 1].astype(F32)
        hi = rpart[k, v, half:rows, :] + frecv[k, 0].astype(F32) + frecv[k, 3].astype(F32)
        out_ref[k * rows:k * rows + half, :] = lo.astype(BF16)
        out_ref[k * rows + half:(k + 1) * rows, :] = hi.astype(BF16)

    both = range(2)
    steps = [(a_send, s) for s in range(WINDOW, min(12, WINDOW + 4))]
    steps += [(a_fin, 0)] + [(b_send, 0, m) for m in both] + [(c_send, 0)]
    steps += [(a_send, s) for s in range(WINDOW + 4, 12)]
    steps += [(a_fin, 1)] + [(b_send, 1, m) for m in both]
    steps += [(b_fwd, 0, m) for m in both] + [(c_send, 1)]
    steps += [(a_fin, 2), (b_send, 2, 0)] + [(b_fwd, 1, m) for m in both]
    steps += [(b_send, 2, 1), (c_send, 2)]
    steps += [(b_core, q, m) for q in both for m in both]
    steps += [
        (b_fwd, 2, 0), (c_fwd, 0), (b_fwd, 2, 1), (b_core, 2, 0), (c_fwd, 1),
        (y_stage, 0), (d_send, 0), (d_send, 1), (c_fwd, 2),
        (b_core, 2, 1), (y_stage, 1), (d_fwd, 0), (d_fwd, 1), (d_send, 2), (d_send, 3),
        (c_fin, 0), (c_fin, 1), (c_fin, 2),
        (pair, 0), (pair, 1), (e2, 0), (e2, 1), (d_fwd, 2), (d_fwd, 3),
        (e3, 0), (e3, 1), (pair, 2), (pair, 3), (e2, 2), (e2, 3), (e4, 0), (e4, 1),
        (res, 0), (res, 1), (e3, 2), (e3, 3), (f_fwd, 0), (f_fwd, 1),
        (e4, 2), (e4, 3), (res, 2), (res, 3), (f_fin, 0), (f_fin, 1), (f_fwd, 2), (f_fwd, 3),
    ]
    steps += [(f_fin, 2), (f_fin, 3)]
    for stage, *at in steps:
        stage(*at)
    for copy in open_sends:
        copy.wait_send()


def local(orbitals, point_owner, point_row, density_tiles, tile_columns, tile_counts):
    rows = BLK // NCH
    half = rows // 2
    vmem = pl.BlockSpec(memory_space=pltpu.VMEM)
    smem = pl.BlockSpec(memory_space=pltpu.SMEM)
    hbm = pl.BlockSpec(memory_space=pl.ANY)
    return pl.pallas_call(
        kernel,
        name="exchange",
        out_shape=jax.ShapeDtypeStruct((BLK, COLS), BF16),
        in_specs=[vmem, smem, smem, hbm, hbm],
        out_specs=vmem,
        scratch_shapes=[
            pltpu.VMEM((1024, COLS), BF16),
            pltpu.VMEM((18, TILE, TILE), BF16),
            pltpu.VMEM((512, 1024), BF16),
            pltpu.VMEM((3, 512, TILE), BF16),
            pltpu.VMEM((3, 512, TILE), BF16),
            pltpu.VMEM((2, 3, 4, BLK, TILE), BF16),
            pltpu.VMEM((24, 128, TILE), BF16),
            pltpu.VMEM((24, 128, TILE), BF16),
            pltpu.VMEM((4, BLK, COLS), BF16),
            pltpu.VMEM((NCH, 2, 4 * rows, TILE), F32),
            pltpu.VMEM((NCH, 4 * rows, TILE), F32),
            pltpu.VMEM((NCH, 4, rows, TILE), BF16),
            pltpu.VMEM((NCH, 3, rows, TILE), BF16),
            pltpu.VMEM((NCH, 2, 4, rows, TILE), BF16),
            pltpu.VMEM((NCH, 4, rows, COLS), F32),
            pltpu.VMEM((NCH, 4, rows, COLS), BF16),
            pltpu.VMEM((NCH, 4, half, COLS), BF16),
            pltpu.VMEM((NCH, 2, half, COLS), BF16),
            pltpu.VMEM((NCH, 2, half, COLS), BF16),
            pltpu.VMEM((3, 16, BLK), F32),
            pltpu.SemaphoreType.DMA((NSEM,)),
            pltpu.SemaphoreType.DMA((NSEM,)),
            pltpu.SemaphoreType.DMA((2,)),
        ],
        compiler_params=pltpu.CompilerParams(
            collective_id=0, has_side_effects=True, vmem_limit_bytes=60 * 2**20
        ),
        cost_estimate=pl.CostEstimate(
            flops=12_000_000_000, bytes_accessed=14_000_000, transcendentals=0
        ),
    )(
        (point_owner[:, 0] * 1024 + point_row).reshape(16, BLK),
        tile_columns,
        tile_counts,
        orbitals,
        density_tiles.reshape(18, TILE, TILE),
    )


def solution(mesh):
    in_specs = (
        P("grid", "band"),
        P(),
        P(),
        P("band", None, None, None),
        P("band", None),
        P("band"),
    )
    return jax.shard_map(
        local, mesh=mesh, in_specs=in_specs, out_specs=P("grid", "band"), check_vma=False
    )
```

```python
import functools

import jax
import jax.numpy as jnp
from jax import lax
from jax.experimental import pallas as pl
from jax.experimental.pallas import tpu as pltpu
from jax.sharding import PartitionSpec as P

MESH = pl.DeviceIdType.MESH
F32 = jnp.float32
BF16 = jnp.bfloat16
NCH = 4
BLK = 256
COLS = 1536
TILE = 512
CAP = 32
NSEM = 200
FORWARDED = 3
WINDOW = 5


def nt(a, b):
    return lax.dot_general(a, b, (((1,), (1,)), ((), ())), preferred_element_type=F32)


def nn(a, b):
    return lax.dot_general(a, b, (((1,), (0,)), ((), ())), preferred_element_type=F32)


def kernel(
    index_ref, cols_ref, counts_ref, orb_hbm, tiles_hbm, out_ref,
    orb, tiles, onehot, slots_out, slots_in, xn, ev0, ev1, yg,
    pch, csend, crecv, ysend, yrecv, sfull, rpart, fsend, frecv, ffwd, fsum, pos,
    ss, rs, ls,
):
    every = (ev0, ev1)
    rows = BLK // NCH
    half = rows // 2
    g = lax.axis_index("grid")
    b = lax.axis_index("band")
    z, x, y, c = g // 4, g % 4, b // 2, b % 2
    o = 1 - c

    def grid_of(zz, xx):
        return (((zz + 4) % 4) * 4 + (xx + 4) % 4, b)

    def y_of(yy):
        return (g, ((yy + 4) % 4) * 2 + c)

    core_peer = (g, y * 2 + o)
    up = lambda v, d: (v + d + 4) % 4

    place = (z, x)

    def ring(mode, d):
        return grid_of(z + d, x) if mode == 0 else grid_of(z, x + d)

    counter = [0]
    open_sends = []

    def send(src, dst, to):
        k = counter[0]
        counter[0] += 1
        copy = pltpu.make_async_remote_copy(
            src_ref=src, dst_ref=dst, send_sem=ss.at[k], recv_sem=rs.at[k],
            device_id=to, device_id_type=MESH,
        )
        copy.start()
        open_sends.append(copy)
        return copy

    bar = pltpu.get_barrier_semaphore()
    for dz in (2, 1, 3, 0):
        for dx in (2, 1, 3, 0):
            if (dz, dx) != (0, 0):
                pl.semaphore_signal(
                    bar, inc=1, device_id=grid_of(z + dz, x + dx), device_id_type=MESH
                )
    for dy in (1, 2, 3):
        pl.semaphore_signal(bar, inc=1, device_id=y_of(y + dy), device_id_type=MESH)
    pl.semaphore_signal(bar, inc=1, device_id=core_peer, device_id_type=MESH)

    load_orb = pltpu.make_async_copy(orb_hbm, orb, ls.at[0])
    load_orb.start()
    load_tiles = pltpu.make_async_copy(tiles_hbm, tiles, ls.at[1])
    load_tiles.start()

    index = index_ref[...]
    owner = index // 1024
    rowf = (index % 1024).astype(F32)
    holder = (owner == g).astype(F32)
    p0 = lax.broadcasted_iota(jnp.int32, (BLK, BLK), 0)
    p1 = lax.broadcasted_iota(jnp.int32, (BLK, BLK), 1)
    before = (p0 < p1).astype(BF16)
    ahead = nn(holder.astype(BF16), before)
    slot_id = lax.broadcasted_iota(jnp.int32, (CAP, BLK), 0).astype(F32)
    grid_row = lax.broadcasted_iota(jnp.int32, (CAP, 1024), 1).astype(F32)
    for i in range(16):
        picked = (ahead[i:i + 1, :] == slot_id) & (holder[i:i + 1, :] > 0.5)
        wanted = jnp.sum(jnp.where(picked, rowf[i:i + 1, :], 0.0), axis=1, keepdims=True)
        onehot[i * CAP:(i + 1) * CAP, :] = (grid_row == wanted).astype(F32).astype(BF16)

    load_orb.wait()
    mine = pl.ds(pl.multiple_of(g * CAP, CAP), CAP)
    groups = (
        ((2, 1), (2, 3), (1, 2), (3, 2)),
        ((2, 0), (0, 2), (2, 2)),
        ((1, 1), (3, 3), (1, 3), (3, 1)),
        ((1, 0), (3, 0), (0, 1), (0, 3)),
    )
    pieces = [(q, group) for q in range(3) for group in groups]
    a_copies = []

    def a_rows(q):
        slots_out[q] = nn(onehot[...], orb[:, q * TILE:(q + 1) * TILE]).astype(BF16)
        slots_in[q, mine, :] = slots_out[q, mine, :]

    def a_send(s):
        if s >= WINDOW:
            for copy in a_copies[s - WINDOW]:
                copy.wait_send()
                open_sends[:] = [other for other in open_sends if other is not copy]
        q, group = pieces[s]
        sent = []
        for dz, dx in group:
            to = grid_of(z + dz, x + dx)
            src = pl.ds(pl.multiple_of(to[0] * CAP, CAP), CAP)
            sent.append(send(slots_out.at[q, src], slots_in.at[q, mine], to))
        a_copies.append(sent)

    a_rows(0)
    pl.semaphore_wait(bar, 19)
    for s in range(min(WINDOW, 4)):
        a_send(s)
    a_rows(1)
    for s in range(4, WINDOW):
        a_send(s)
    a_rows(2)

    pos[0] = (index % 16).astype(F32)
    pos[1] = (index // 16 % 16).astype(F32)
    pos[2] = (index // 256).astype(F32)
    own_row = (index_ref[pl.ds(g, 1), :] // 1024).astype(F32)
    own_col = jnp.sum(jnp.where(p0 == p1, own_row, 0.0), axis=1, keepdims=True)
    rank = jnp.sum(
        jnp.where((own_row == own_col) & (p1 < p0), 1.0, 0.0), axis=1, keepdims=True
    )
    flat = own_col * CAP + rank
    slot_no = lax.broadcasted_iota(jnp.int32, (BLK, 16 * CAP), 1).astype(F32)
    unpermute = (slot_no == flat).astype(F32).astype(BF16)

    st = {}

    def a_fin(q):
        for group in a_copies[4 * q:4 * q + 4]:
            for copy in group:
                copy.wait_recv()
        points = nn(unpermute, slots_in[q]).astype(BF16)
        xn[0, q, x] = points
        xn[1, q, z] = points
        for m in range(2):
            every[m][c * 12 + q * 4 + y] = points[m * 128:(m + 1) * 128, :]

    def b_send(q, m):
        src = every[m].at[c * 12 + q * 4 + y]
        ways = (1, 3) if q < FORWARDED else (2, 1, 3)
        st["b", q, m] = [send(src, src, y_of(y + d)) for d in ways]

    def b_fwd(q, m):
        plus, minus = st["b", q, m]
        plus.wait_recv()
        src = every[m].at[c * 12 + q * 4 + up(y, -1), pl.ds(0, 64)]
        forwarded = [send(src, src, y_of(y + 1))]
        minus.wait_recv()
        src = every[m].at[c * 12 + q * 4 + up(y, 1), pl.ds(64, 64)]
        st["b", q, m] = forwarded + [send(src, src, y_of(y - 1))]

    def b_core(q, m):
        for copy in st["b", q, m]:
            copy.wait_recv()
        src = every[m].at[pl.ds(c * 12 + q * 4, 4)]
        st["bc", q, m] = send(src, src, core_peer)

    def y_stage(m):
        for q in range(3):
            st["bc", q, m].wait_recv()
        if m == 0:
            load_tiles.wait()
        for r in range(3):
            acc = jnp.zeros((128, TILE), F32)
            count = counts_ref[r]
            for s in range(6):
                col = cols_ref[r, s]
                block = every[m][(col // 3 % 2) * 12 + (col % 3) * 4 + col // 6]
                if s > 0:
                    keep = (count > s).astype(F32)
                    block = block * keep.astype(BF16)
                acc = acc + nt(block, tiles[r * 6 + s])
            acc = acc.astype(BF16)
            cut = slice(r * TILE, (r + 1) * TILE)
            yg[z, m * 128:m * 128 + 64, cut] = acc[:64]
            yg[x, m * 128 + 64:m * 128 + 128, cut] = acc[64:]

    def place_of(k):
        return place[k % 2]

    def c_send(q):
        for mode in range(2):
            v = place[1 - mode]
            src = xn.at[mode, q, v]
            st["c", q, mode] = [send(src, src, ring(1 - mode, d)) for d in (1, -1)]

    def c_fwd(q):
        for mode in range(2):
            v = place[1 - mode]
            plus, minus = st["c", q, mode]
            plus.wait_recv()
            src = xn.at[mode, q, up(v, -1), pl.ds(0, 128)]
            ahead_copy = send(src, src, ring(1 - mode, 1))
            minus.wait_recv()
            src = xn.at[mode, q, up(v, 1), pl.ds(128, 128)]
            st["cf", q, mode] = (ahead_copy, send(src, src, ring(1 - mode, -1)))

    def c_fin(q):
        for mode in range(2):
            for copy in st["cf", q, mode]:
                copy.wait_recv()

    def d_send(k):
        src = yg.at[place_of(k), pl.ds(k * rows, rows)]
        st["dp", k] = send(src, src, ring(k % 2, 1))
        st["dm", k] = send(src, src, ring(k % 2, -1))

    def d_fwd(k):
        st["dp", k].wait_recv()
        src = yg.at[up(place_of(k), -1), pl.ds(k * rows, half)]
        st["dfp", k] = send(src, src, ring(k % 2, 1))
        st["dm", k].wait_recv()
        src = yg.at[up(place_of(k), 1), pl.ds(k * rows + half, half)]
        st["dfm", k] = send(src, src, ring(k % 2, -1))

    def pair(k):
        st["dfp", k].wait_recv()
        st["dfm", k].wait_recv()
        mode = k % 2
        for h in (o, c):
            total = None
            for q in range(3):
                lhs = yg[:, k * rows:(k + 1) * rows, q * TILE:(q + 1) * TILE]
                rhs = xn[mode, q, pl.ds(2 * h, 2)]
                term = nt(lhs.reshape(4 * rows, TILE), rhs.reshape(2 * BLK, TILE))
                total = term if total is None else total + term
            if h is o:
                csend[k] = total.astype(BF16)
                st["e1", k] = send(csend.at[k], crecv.at[k], core_peer)
            else:
                pch[k] = total

    def e2(k):
        st["e1", k].wait_recv()
        total = pch[k] + crecv[k].astype(F32)
        pch[k] = total
        ysend[k] = total.astype(BF16).reshape(4, rows, TILE)
        for d in (2, 1, 3):
            st["e2", k, d] = send(
                ysend.at[k, up(y, d)], yrecv.at[k, d - 1], y_of(y + d)
            )

    def e3(k):
        part = pl.ds(pl.multiple_of(y * rows, rows), rows)
        total = pch[k, part, :]
        for d in (1, 2, 3):
            st["e2", k, d].wait_recv()
            total = total + yrecv[k, d - 1].astype(F32)
        eye0 = lax.broadcasted_iota(jnp.int32, (rows, BLK), 0) + k * rows
        eye1 = lax.broadcasted_iota(jnp.int32, (rows, BLK), 1)
        eye = eye0 == eye1
        mu_block = y * 4 + x if k % 2 == 0 else z * 4 + y
        sides = []
        mu_at = [
            jnp.sum(jnp.where(eye, pos[a, pl.ds(mu_block, 1), :], 0.0), axis=1, keepdims=True)
            for a in range(3)
        ]
        for h in range(2):
            nu_block = z * 4 + 2 * c + h if k % 2 == 0 else (2 * c + h) * 4 + x
            dist = jnp.ones((rows, BLK), F32)
            for a in range(3):
                delta = mu_at[a] - pos[a, pl.ds(nu_block, 1), :]
                dist = dist + delta * delta
            sides.append(lax.rsqrt(dist))
        kern = jnp.concatenate(sides, axis=1)
        sfull[k, c, y] = (total * kern).astype(BF16)
        src = sfull.at[k, c, y]
        for d in (2, 1, 3):
            st["e3", k, d] = send(src, src, y_of(y + d))

    def e4(k):
        for d in (1, 2, 3):
            st["e3", k, d].wait_recv()
        src = sfull.at[k, c]
        st["e4", k] = send(src, src, core_peer)

    def res(k):
        st["e4", k].wait_recv()
        mode = k % 2
        lhs = [sfull[k, h].reshape(4 * rows, 2 * BLK) for h in range(2)]
        for q in range(3):
            total = nn(lhs[0], xn[mode, q, 0:2].reshape(2 * BLK, TILE))
            total = total + nn(lhs[1], xn[mode, q, 2:4].reshape(2 * BLK, TILE))
            cut = slice(q * TILE, (q + 1) * TILE)
            rpart[k, :, :, cut] = total.reshape(4, rows, TILE)
            fsend[k, :, :, cut] = total.astype(BF16).reshape(4, rows, TILE)
        v = place_of(k)
        far_v, up_v, dn_v = up(v, 2), up(v, 1), up(v, -1)
        lo, hi = pl.ds(0, half), pl.ds(half, half)
        st["fp", k] = send(fsend.at[k, far_v, lo], ffwd.at[k, 0], ring(mode, 1))
        st["fm", k] = send(fsend.at[k, far_v, hi], ffwd.at[k, 1], ring(mode, -1))
        st["fdp", k] = send(fsend.at[k, up_v, hi], frecv.at[k, 0], ring(mode, 1))
        st["fdm", k] = send(fsend.at[k, dn_v, lo], frecv.at[k, 1], ring(mode, -1))

    def f_fwd(k):
        up_v, dn_v = up(place_of(k), 1), up(place_of(k), -1)
        st["fp", k].wait_recv()
        fsum[k, 0] = (rpart[k, up_v, 0:half, :] + ffwd[k, 0].astype(F32)).astype(BF16)
        st["fsp", k] = send(fsum.at[k, 0], frecv.at[k, 2], ring(k % 2, 1))
        st["fm", k].wait_recv()
        fsum[k, 1] = (rpart[k, dn_v, half:rows, :] + ffwd[k, 1].astype(F32)).astype(BF16)
        st["fsm", k] = send(fsum.at[k, 1], frecv.at[k, 3], ring(k % 2, -1))

    def f_fin(k):
        v = place_of(k)
        for name in ("fdp", "fdm", "fsp", "fsm"):
            st[name, k].wait_recv()
        lo = rpart[k, v, 0:half, :] + frecv[k, 2].astype(F32) + frecv[k, 1].astype(F32)
        hi = rpart[k, v, half:rows, :] + frecv[k, 0].astype(F32) + frecv[k, 3].astype(F32)
        out_ref[k * rows:k * rows + half, :] = lo.astype(BF16)
        out_ref[k * rows + half:(k + 1) * rows, :] = hi.astype(BF16)

    both = range(2)
    steps = [(a_send, s) for s in range(WINDOW, min(12, WINDOW + 4))]
    steps += [(a_fin, 0)] + [(b_send, 0, m) for m in both]
    steps += [(a_send, s) for s in range(WINDOW + 4, 12)]
    steps += [(a_fin, 1)] + [(b_send, 1, m) for m in both]
    steps += [(b_fwd, 0, m) for m in both]
    steps += [(a_fin, 2), (b_send, 2, 0), (c_send, 0), (c_send, 1)] + [(b_fwd, 1, m) for m in both]
    steps += [(b_send, 2, 1), (c_send, 2)]
    steps += [(b_core, q, m) for q in both for m in both]
    steps += [
        (b_fwd, 2, 0), (c_fwd, 0), (b_fwd, 2, 1), (b_core, 2, 0), (c_fwd, 1),
        (y_stage, 0), (d_send, 0), (d_send, 1), (c_fwd, 2),
        (b_core, 2, 1), (y_stage, 1), (d_fwd, 0), (d_fwd, 1), (d_send, 2), (d_send, 3),
        (c_fin, 0), (c_fin, 1), (c_fin, 2),
        (pair, 0), (pair, 1), (e2, 0), (e2, 1), (d_fwd, 2), (d_fwd, 3),
        (e3, 0), (e3, 1), (pair, 2), (pair, 3), (e2, 2), (e4, 0), (e2, 3), (e4, 1),
        (res, 0), (res, 1), (e3, 2), (e3, 3), (f_fwd, 0), (f_fwd, 1),
        (e4, 2), (e4, 3), (res, 2), (res, 3), (f_fin, 0), (f_fin, 1), (f_fwd, 2), (f_fwd, 3),
    ]
    steps += [(f_fin, 2), (f_fin, 3)]
    for stage, *at in steps:
        stage(*at)
    for copy in open_sends:
        copy.wait_send()


def local(orbitals, point_owner, point_row, density_tiles, tile_columns, tile_counts):
    rows = BLK // NCH
    half = rows // 2
    vmem = pl.BlockSpec(memory_space=pltpu.VMEM)
    smem = pl.BlockSpec(memory_space=pltpu.SMEM)
    hbm = pl.BlockSpec(memory_space=pl.ANY)
    return pl.pallas_call(
        kernel,
        name="exchange",
        out_shape=jax.ShapeDtypeStruct((BLK, COLS), BF16),
        in_specs=[vmem, smem, smem, hbm, hbm],
        out_specs=vmem,
        scratch_shapes=[
            pltpu.VMEM((1024, COLS), BF16),
            pltpu.VMEM((18, TILE, TILE), BF16),
            pltpu.VMEM((512, 1024), BF16),
            pltpu.VMEM((3, 512, TILE), BF16),
            pltpu.VMEM((3, 512, TILE), BF16),
            pltpu.VMEM((2, 3, 4, BLK, TILE), BF16),
            pltpu.VMEM((24, 128, TILE), BF16),
            pltpu.VMEM((24, 128, TILE), BF16),
            pltpu.VMEM((4, BLK, COLS), BF16),
            pltpu.VMEM((NCH, 4 * rows, TILE), F32),
            pltpu.VMEM((NCH, 4 * rows, TILE), BF16),
            pltpu.VMEM((NCH, 4 * rows, TILE), BF16),
            pltpu.VMEM((NCH, 4, rows, TILE), BF16),
            pltpu.VMEM((NCH, 3, rows, TILE), BF16),
            pltpu.VMEM((NCH, 2, 4, rows, TILE), BF16),
            pltpu.VMEM((NCH, 4, rows, COLS), F32),
            pltpu.VMEM((NCH, 4, rows, COLS), BF16),
            pltpu.VMEM((NCH, 4, half, COLS), BF16),
            pltpu.VMEM((NCH, 2, half, COLS), BF16),
            pltpu.VMEM((NCH, 2, half, COLS), BF16),
            pltpu.VMEM((3, 16, BLK), F32),
            pltpu.SemaphoreType.DMA((NSEM,)),
            pltpu.SemaphoreType.DMA((NSEM,)),
            pltpu.SemaphoreType.DMA((2,)),
        ],
        compiler_params=pltpu.CompilerParams(
            collective_id=0, has_side_effects=True, vmem_limit_bytes=60 * 2**20
        ),
        cost_estimate=pl.CostEstimate(
            flops=12_000_000_000, bytes_accessed=14_000_000, transcendentals=0
        ),
    )(
        (point_owner[:, 0] * 1024 + point_row).reshape(16, BLK),
        tile_columns,
        tile_counts,
        orbitals,
        density_tiles.reshape(18, TILE, TILE),
    )


def solution(mesh):
    in_specs = (
        P("grid", "band"),
        P(),
        P(),
        P("band", None, None, None),
        P("band", None),
        P("band"),
    )
    return jax.shard_map(
        local, mesh=mesh, in_specs=in_specs, out_specs=P("grid", "band"), check_vma=False
    )
```
